1024 devices in a mesh: inner: 8 (over x, z_hi), outer: 128 (over z_lo, y, core).
Axes of the slice: x: 4, y: 8, z: 16 (z_hi: 2, z_lo: 8; z = z_hi * 8 + z_lo), core: 2. Of those that a mesh axis runs over, the one named last changes fastest.
Arguments:
- aggregated_picture_vectors: bfloat16 [128, 384, 1152], P('outer'), may hold values from -6 to 6
- raw_image_embedding: float32 [128, 384, 1152], P('outer'), may hold values from -0.4375 to 0.4375
- raw_caption_embedding: bfloat16 [128, 384, 1152], P('outer', 'inner'), may hold values from -0.4375 to 0.4375
- matching_caption_slot: int32 [128, 384], P('outer'), may hold values from 0 to 383, each once within a row
- standardize_factor: float32 [1152], replicated, may hold values from 0.5 to 1.5
- standardize_shift: float32 [1152], replicated, may hold values from -3 to 3
- hidden_projection_matrix: bfloat16 [1152, 4304], P(None, 'inner'), may hold values from -0.1875 to 0.1875
- hidden_shift_vector: float32 [4304], P('inner'), may hold values from -3 to 3
- return_projection_matrix: bfloat16 [4304, 1152], P('inner'), may hold values from -0.09375 to 0.09375
- sharpness_factor: float32 [1], replicated, may hold values from 4 to 12
- similarity_shift: float32 [1], replicated, may hold values from -6 to -2
Outputs:
- d_pooled: bfloat16 [128, 384, 1152], P('outer', 'inner')
- d_text: bfloat16 [128, 384, 1152], P('outer', 'inner')
The draws below stay inside these ranges and needn't reach their ends.
Inputs may be any that keep to these rules, and one draw needn't show every extreme that they name: `matching_caption_slot`: within each group every position appears once.
All inputs are finite; a program needn't handle non-finite values.
Results may differ from the reference program's by a relative error of at most 0.023.
Values may be sent and summed in bfloat16 or wider, within the bound.
No kernel may reach another device: no remote copies, remote signals or barrier semaphores. Data moves between devices by JAX's collectives and lax.ppermute only.
A program may use at most 32 MiB of HBM per device.

```python
import jax
import jax.numpy as jnp
from jax import lax

D = 1152
FF = 4304
TXT_DEV = 48
STEPS = 8
IMG_GROUP = 384
N_INNER = 8
N_OUTER = 128


def block_scale(stream_key, extent, split, least, high):
    factor_of, own = 1.0, jax.random.fold_in(stream_key, 6)
    for axis_at, blocks in split:
        steps = jnp.exp(jax.random.uniform(jax.random.fold_in(own, axis_at), (blocks,), jnp.float32, least / len(split), high / len(split)))
        factor_of = factor_of * jnp.repeat(steps, extent[axis_at] // blocks).reshape([-1 if axis == axis_at else 1 for axis in range(len(extent))])
    return factor_of


def bell_draw(stream_key, extent, spread, limit, split=(), kind=jnp.bfloat16):
    loudness = block_scale(stream_key, extent, split, -0.22, 0.18) if split else 1.0
    entries = jax.random.normal(stream_key, extent, jnp.float32) * spread * loudness
    return jnp.minimum(jnp.maximum(entries, -limit), limit).astype(kind)


def setup_inputs(seed: int = 0) -> dict:
    keys = jax.random.split(jax.random.key(seed), 12)
    aggregated_picture_vectors = bell_draw(keys[0], (N_OUTER, IMG_GROUP, D), 1.0, 6.0, ((0, 128),))
    raw_image_embedding = bell_draw(keys[1], (N_OUTER, IMG_GROUP, D), 0.03, 0.4375, ((0, 128),), jnp.float32)
    raw_caption_embedding = bell_draw(keys[2], (N_OUTER, IMG_GROUP, D), 0.03, 0.4375, ((0, 128), (1, 8)))
    matching_caption_slot = jax.vmap(lambda own: jax.random.permutation(own, IMG_GROUP))(jax.random.split(keys[3], N_OUTER)).reshape((N_OUTER, IMG_GROUP)).astype(jnp.int32)
    standardize_factor = jnp.clip(1.0 + 0.1 * jax.random.normal(keys[4], (D,), jnp.float32), 0.5, 1.5)
    standardize_shift = bell_draw(keys[5], (D,), 0.5, 3.0, (), jnp.float32)
    hidden_projection_matrix = bell_draw(keys[6], (D, FF), D ** -0.5, 0.1875, ((1, 8),))
    hidden_shift_vector = bell_draw(keys[7], (FF,), 0.5, 3.0, ((0, 8),), jnp.float32)
    return_projection_matrix = bell_draw(keys[8], (FF, D), FF ** -0.5, 0.09375, ((0, 8),))
    sharpness_factor = jnp.clip(jax.random.uniform(keys[9], (1,), jnp.float32, 4.0, 12.0), 4.0, 12.0)
    similarity_shift = jnp.clip(jax.random.uniform(keys[10], (1,), jnp.float32, -6.0, -2.0), -6.0, -2.0)
    return dict(aggregated_picture_vectors=aggregated_picture_vectors, raw_image_embedding=raw_image_embedding, raw_caption_embedding=raw_caption_embedding, matching_caption_slot=matching_caption_slot, standardize_factor=standardize_factor, standardize_shift=standardize_shift, hidden_projection_matrix=hidden_projection_matrix, hidden_shift_vector=hidden_shift_vector, return_projection_matrix=return_projection_matrix, sharpness_factor=sharpness_factor, similarity_shift=similarity_shift)


SQRT_TWO_PI = 0.7978845608028654
CUBIC = 0.044715
EPSILON = 1e-06

def gelu_slope(pre_values):
    tangent = jnp.tanh(SQRT_TWO_PI * (pre_values + CUBIC * pre_values ** 3))
    return 0.5 * (1.0 + tangent) + 0.5 * pre_values * (1.0 - tangent * tangent) * SQRT_TWO_PI * (1.0 + 3.0 * CUBIC * pre_values * pre_values)

def unit_rows(row_block):
    row_norms = jnp.sqrt(lax.optimization_barrier(jnp.sum(row_block * row_block, axis=-1, keepdims=True)))
    return (row_block / row_norms, row_norms)

def couple_sensitivity(picture_tile, caption_tile, agreement_signs, similarity_multiplier, similarity_displacement, leading_entry):
    similarity_matrix = similarity_multiplier * jnp.dot(picture_tile, caption_tile.T, preferred_element_type=jnp.float32) + similarity_displacement
    if leading_entry:
        labels = jnp.where(agreement_signs, 1.0, -1.0).astype(jnp.float32)
    else:
        labels = -jnp.ones_like(similarity_matrix)
    return (-labels * jax.nn.sigmoid(-labels * similarity_matrix)).astype(jnp.bfloat16)

def layer_back(pooled_rows, upstream_bf, standardize_factor, standardize_shift, hidden_projection_matrix, hidden_shift_vector, return_projection_matrix):
    features = pooled_rows.astype(jnp.float32)
    row_mean = lax.optimization_barrier(jnp.mean(features, axis=-1, keepdims=True))
    centred = features - row_mean
    variance = lax.optimization_barrier(jnp.mean(centred * centred, axis=-1, keepdims=True))
    inv_std = lax.rsqrt(variance + EPSILON)
    normalized = centred * inv_std
    layer_in = (normalized * standardize_factor + standardize_shift).astype(jnp.bfloat16)
    pre_act = jnp.dot(layer_in, hidden_projection_matrix, preferred_element_type=jnp.float32) + hidden_shift_vector
    back_act = jnp.dot(upstream_bf, return_projection_matrix.T, preferred_element_type=jnp.float32)
    act_grad = (back_act * gelu_slope(pre_act)).astype(jnp.bfloat16)
    back_norm = jnp.dot(act_grad, hidden_projection_matrix.T, preferred_element_type=jnp.float32) * standardize_factor
    first_mean = lax.optimization_barrier(jnp.mean(back_norm, axis=-1, keepdims=True))
    second_mean = lax.optimization_barrier(jnp.mean(back_norm * normalized, axis=-1, keepdims=True))
    return (back_norm - first_mean - normalized * second_mean) * inv_std

def reference(aggregated_picture_vectors, raw_image_embedding, raw_caption_embedding, matching_caption_slot, standardize_factor, standardize_shift, hidden_projection_matrix, hidden_shift_vector, return_projection_matrix, sharpness_factor, similarity_shift):
    similarity_multiplier = sharpness_factor[0]
    similarity_displacement = similarity_shift[0]
    image_units, image_norms = unit_rows(raw_image_embedding)
    picture_halfprec = image_units.astype(jnp.bfloat16)
    text_units, text_norms = unit_rows(raw_caption_embedding.astype(jnp.float32))
    text_bf = text_units.astype(jnp.bfloat16)
    text_ids = jnp.arange(IMG_GROUP, dtype=jnp.int32)
    hidden_each = FF // N_INNER

    def image_side(group_id):
        local_pictures = lax.dynamic_index_in_dim(picture_halfprec, group_id, 0, keepdims=False)
        own_units = lax.dynamic_index_in_dim(image_units, group_id, 0, keepdims=False)
        own_norms = lax.dynamic_index_in_dim(image_norms, group_id, 0, keepdims=False)
        own_pos = lax.dynamic_index_in_dim(matching_caption_slot, group_id, 0, keepdims=False)
        agreement_signs = own_pos[:, None] == text_ids[None, :]
        running_total = jnp.zeros((N_INNER, IMG_GROUP, D), jnp.float32)
        for starting_position in range(STEPS):
            source = ((group_id - starting_position) % N_OUTER).astype(jnp.int32)
            caption_tile = lax.dynamic_index_in_dim(text_bf, source, 0, keepdims=False)
            couple_derivative = couple_sensitivity(local_pictures, caption_tile, agreement_signs, similarity_multiplier, similarity_displacement, starting_position == 0)
            divided_derivative = couple_derivative.reshape(IMG_GROUP, N_INNER, TXT_DEV).astype(jnp.float32)
            divided_captions = caption_tile.reshape(N_INNER, TXT_DEV, D).astype(jnp.float32)
            running_total = running_total + similarity_multiplier * jnp.einsum('qsv,svm->sqm', divided_derivative, divided_captions)
        rounded = lax.optimization_barrier(running_total.astype(jnp.bfloat16))
        image_grad = lax.optimization_barrier(jnp.sum(rounded.astype(jnp.float32), axis=0))
        upstream = (image_grad - own_units * lax.optimization_barrier(jnp.sum(own_units * image_grad, axis=-1, keepdims=True))) / own_norms
        upstream_bf = upstream.astype(jnp.bfloat16)
        own_pooled = lax.dynamic_index_in_dim(aggregated_picture_vectors, group_id, 0, keepdims=False)
        total_sum = jnp.zeros((IMG_GROUP, D), jnp.float32)
        for shard in range(N_INNER):
            low = shard * hidden_each
            partial_value = layer_back(own_pooled, upstream_bf, standardize_factor, standardize_shift, hidden_projection_matrix[:, low:low + hidden_each], hidden_shift_vector[low:low + hidden_each], return_projection_matrix[low:low + hidden_each, :])
            partial_bf = lax.optimization_barrier(partial_value.astype(jnp.bfloat16))
            total_sum = total_sum + partial_bf.astype(jnp.float32)
        return (upstream + total_sum).astype(jnp.bfloat16)

    def text_side(group_id):
        local_captions = lax.dynamic_index_in_dim(text_bf, group_id, 0, keepdims=False)
        own_units = lax.dynamic_index_in_dim(text_units, group_id, 0, keepdims=False)
        own_norms = lax.dynamic_index_in_dim(text_norms, group_id, 0, keepdims=False)
        running_total = jnp.zeros((IMG_GROUP, D), jnp.float32)
        for starting_position in range(STEPS):
            source = ((group_id + starting_position) % N_OUTER).astype(jnp.int32)
            picture_tile = lax.dynamic_index_in_dim(picture_halfprec, source, 0, keepdims=False)
            source_pos = lax.dynamic_index_in_dim(matching_caption_slot, source, 0, keepdims=False)
            agreement_signs = source_pos[:, None] == text_ids[None, :]
            couple_derivative = couple_sensitivity(picture_tile, local_captions, agreement_signs, similarity_multiplier, similarity_displacement, starting_position == 0)
            running_total = running_total + similarity_multiplier * jnp.dot(couple_derivative.T, picture_tile, preferred_element_type=jnp.float32)
        text_grad = (running_total - own_units * lax.optimization_barrier(jnp.sum(own_units * running_total, axis=-1, keepdims=True))) / own_norms
        return text_grad.astype(jnp.bfloat16)
    groups = jnp.arange(N_OUTER, dtype=jnp.int32)
    d_pooled = lax.map(image_side, groups)
    d_text = lax.map(text_side, groups)
    return (d_pooled, d_text)
```

```python
import jax
import jax.numpy as jnp
from jax import lax
from jax.sharding import Mesh
from jax.sharding import PartitionSpec as P

SQRT_TWO_PI = 0.7978845608028654
CUBIC = 0.044715
EPSILON = 1e-06

AXES = (("x", 4), ("zh", 2), ("zl", 8), ("y", 8), ("core", 2))
SIZE = dict(AXES)
INNER = ("x", "zh")
OUTER = ("zl", "y", "core")
RING = ("zh", "zl", "y")
BF = jnp.bfloat16
F32 = jnp.float32


def permute(value, axes, target):
    count = 1
    for axis in axes:
        count *= SIZE[axis]
    return lax.ppermute(value, axes, [(source, target(source) % count) for source in range(count)])


def ring_shift(value, steps):
    return permute(value, RING, lambda at: at + steps)


def core_swap(value):
    return permute(value, ("core",), lambda at: 1 - at)


def z_swap(value):
    return permute(value, ("zh",), lambda at: 1 - at)


def far_forward(value):
    return permute(value, RING + ("core",), lambda at: at + 1 if at % 2 == 0 else at + 3)


def far_back(value):
    return permute(value, RING + ("core",), lambda at: at - 1 if at % 2 == 1 else at - 7)


def dot_nt(a, b):
    return lax.dot_general(a, b, (((1,), (1,)), ((), ())), preferred_element_type=F32)


def dot_tn(a, b):
    return lax.dot_general(a, b, (((0,), (0,)), ((), ())), preferred_element_type=F32)


def gelu_slope(pre_values):
    tangent = jnp.tanh(SQRT_TWO_PI * (pre_values + CUBIC * pre_values**3))
    return 0.5 * (1.0 + tangent) + 0.5 * pre_values * (1.0 - tangent * tangent) * SQRT_TWO_PI * (
        1.0 + 3.0 * CUBIC * pre_values * pre_values
    )


def unit_rows(row_block):
    row_norms = jnp.sqrt(jnp.sum(row_block * row_block, axis=-1, keepdims=True))
    return (row_block / row_norms, row_norms)


def norm_back(grad, units, norms):
    return (grad - units * jnp.sum(units * grad, axis=-1, keepdims=True)) / norms


def rows_of(value, start, count):
    return lax.dynamic_slice_in_dim(value, start, count, 0)


def local(
    aggregated_picture_vectors,
    raw_image_embedding,
    raw_caption_embedding,
    matching_caption_slot,
    standardize_factor,
    standardize_shift,
    hidden_projection_matrix,
    hidden_shift_vector,
    return_projection_matrix,
    sharpness_factor,
    similarity_shift,
):
    scale = sharpness_factor[0]
    shift = similarity_shift[0]
    x = lax.axis_index("x")
    zh = lax.axis_index("zh")
    core = lax.axis_index("core")
    text_units, text_norms = unit_rows(raw_caption_embedding[0].astype(F32))
    own_text = text_units.astype(BF)
    rows = own_text.shape[0]

    one = ring_shift(own_text, 1)
    two = ring_shift(own_text, 2)
    three = ring_shift(one, 2)
    far = far_forward(jnp.where(core == 0, own_text, two))
    same = jnp.concatenate([one, two, three], 0)
    other = core_swap(same)

    raw_image = raw_image_embedding[0]
    image_units, _ = unit_rows(raw_image)
    image_bf = image_units.astype(BF)
    texts = jnp.concatenate([own_text, far, same, other], 0)
    logits = scale * dot_nt(image_bf, texts) + shift
    columns = jnp.arange(texts.shape[0], dtype=jnp.int32)
    ids = jnp.where(columns < rows, (x * 2 + zh) * rows + columns, -1)
    match = matching_caption_slot[0][:, None] == ids[None, :]
    chance = jax.nn.sigmoid(jnp.where(match, -logits, logits))
    pair_grad = jnp.where(match, -chance, chance).astype(BF)
    image_part = (scale * jnp.dot(pair_grad, texts, preferred_element_type=F32)).astype(BF)
    text_parts = (scale * dot_tn(pair_grad, image_bf)).astype(BF)

    by_x = lax.all_to_all(image_part, "x", 0, 0, tiled=True)
    own = 2 * rows
    half = jnp.sum(by_x.reshape(4, own, -1).astype(F32), 0).astype(BF)
    image_grad = half.astype(F32) + z_swap(half).astype(F32)
    own_raw = rows_of(raw_image, x * own, own)
    own_units, own_norms = unit_rows(own_raw)
    upstream = norm_back(image_grad, own_units, own_norms)
    upstream_bf = lax.all_gather(upstream.astype(BF), "x", axis=0, tiled=True)

    parts, half = lax.optimization_barrier((text_parts, half))
    own_part, far_part = parts[:rows], parts[rows : 2 * rows]
    same_part, other_part = parts[2 * rows : 5 * rows], parts[5 * rows :]
    met = (same_part.astype(F32) + core_swap(other_part).astype(F32)).astype(BF)
    text_grad = (
        own_part.astype(F32)
        + far_back(far_part).astype(F32)
        + ring_shift(met[:rows], -1).astype(F32)
        + ring_shift(met[rows : 2 * rows], -2).astype(F32)
        + ring_shift(met[2 * rows :], -3).astype(F32)
    )
    d_text = norm_back(text_grad, text_units, text_norms).astype(BF)[None]

    features = aggregated_picture_vectors[0].astype(F32)
    centred = features - jnp.mean(features, axis=-1, keepdims=True)
    inv_std = lax.rsqrt(jnp.mean(centred * centred, axis=-1, keepdims=True) + EPSILON)
    normalized = centred * inv_std
    layer_in = (normalized * standardize_factor + standardize_shift).astype(BF)
    pre_act = jnp.dot(layer_in, hidden_projection_matrix, preferred_element_type=F32) + hidden_shift_vector
    slope = gelu_slope(pre_act)
    back_act = dot_nt(upstream_bf, return_projection_matrix)
    act_grad = (back_act * slope).astype(BF)
    back_norm = dot_nt(act_grad, hidden_projection_matrix) * standardize_factor
    first_mean = jnp.mean(back_norm, axis=-1, keepdims=True)
    second_mean = jnp.mean(back_norm * normalized, axis=-1, keepdims=True)
    ln_part = ((back_norm - first_mean - normalized * second_mean) * inv_std).astype(BF)

    parts_x = lax.all_to_all(ln_part, "x", 0, 0, tiled=True)
    half_sum = jnp.sum(parts_x.reshape(4, own, -1).astype(F32), 0)
    kept = rows_of(half_sum, zh * rows, rows)
    sent = rows_of(half_sum, (1 - zh) * rows, rows).astype(BF)
    d_pooled = rows_of(upstream, zh * rows, rows) + kept + z_swap(sent).astype(F32)
    return (d_pooled.astype(BF)[None], d_text)


def solution(mesh):
    fine = Mesh(mesh.devices.reshape([size for _, size in AXES]), [name for name, _ in AXES])
    placed = (
        P(OUTER, None, None),
        P(OUTER, None, None),
        P(OUTER, INNER, None),
        P(OUTER, None),
        P(),
        P(),
        P(None, INNER),
        P(INNER),
        P(INNER, None),
        P(),
        P(),
    )
    return jax.shard_map(
        local,
        mesh=fine,
        in_specs=placed,
        out_specs=(P(OUTER, INNER, None), P(OUTER, INNER, None)),
        check_vma=False,
    )
```

```python
import jax
import jax.numpy as jnp
from jax import lax
from jax.sharding import Mesh
from jax.sharding import PartitionSpec as P

SQRT_TWO_PI = 0.7978845608028654
CUBIC = 0.044715
EPSILON = 1e-06

AXES = (("x", 4), ("zh", 2), ("zl", 8), ("y", 8), ("core", 2))
SIZE = dict(AXES)
INNER = ("x", "zh")
OUTER = ("zl", "y", "core")
RING = ("zh", "zl", "y")
PIECE = 72
HALF = 8 * PIECE
BF = jnp.bfloat16
F32 = jnp.float32


def permute(value, axes, target):
    count = 1
    for axis in axes:
        count *= SIZE[axis]
    return lax.ppermute(value, axes, [(source, target(source) % count) for source in range(count)])


def ring_shift(value, steps):
    return permute(value, RING, lambda at: at + steps)


def core_swap(value):
    return permute(value, ("core",), lambda at: 1 - at)


def z_swap(value):
    return permute(value, ("zh",), lambda at: 1 - at)


def far_forward(value):
    return permute(value, RING + ("core",), lambda at: at + 1 if at % 2 == 0 else at + 7)


def far_back(value):
    return permute(value, RING + ("core",), lambda at: at - 1 if at % 2 == 1 else at - 7)


def dot_nt(a, b):
    return lax.dot_general(a, b, (((1,), (1,)), ((), ())), preferred_element_type=F32)


def dot_tn(a, b):
    return lax.dot_general(a, b, (((0,), (0,)), ((), ())), preferred_element_type=F32)


def gelu_slope(pre_values):
    tangent = jnp.tanh(SQRT_TWO_PI * (pre_values + CUBIC * pre_values**3))
    return 0.5 * (1.0 + tangent) + 0.5 * pre_values * (1.0 - tangent * tangent) * SQRT_TWO_PI * (
        1.0 + 3.0 * CUBIC * pre_values * pre_values
    )


def unit_rows(row_block):
    row_norms = jnp.sqrt(jnp.sum(row_block * row_block, axis=-1, keepdims=True))
    return (row_block / row_norms, row_norms)


def norm_back(grad, units, norms):
    return (grad - units * jnp.sum(units * grad, axis=-1, keepdims=True)) / norms


def rows_of(value, start, count):
    return lax.dynamic_slice_in_dim(value, start, count, 0)


def local(
    aggregated_picture_vectors,
    raw_image_embedding,
    raw_caption_embedding,
    matching_caption_slot,
    standardize_factor,
    standardize_shift,
    hidden_projection_matrix,
    hidden_shift_vector,
    return_projection_matrix,
    sharpness_factor,
    similarity_shift,
):
    scale = sharpness_factor[0]
    shift = similarity_shift[0]
    x = lax.axis_index("x")
    zh = lax.axis_index("zh")
    piece = lax.axis_index("y") * 2 + lax.axis_index("core")
    hidden = hidden_shift_vector.shape[0]

    picks = jnp.arange(PIECE, dtype=jnp.int32)[:, None] + piece * PIECE
    units_at = jnp.arange(hidden, dtype=jnp.int32)[None, :]
    weight_piece = dot_nt((picks == units_at).astype(BF), hidden_projection_matrix) + jnp.dot(
        (picks - HALF == units_at).astype(BF), return_projection_matrix, preferred_element_type=F32
    )
    high = lax.reduce_precision(hidden_shift_vector, 8, 7)
    middle = lax.reduce_precision(hidden_shift_vector - high, 8, 7)
    low = hidden_shift_vector - high - middle
    for at, term in enumerate((high, middle, low)):
        line = jnp.pad(term, (0, weight_piece.shape[1] - hidden))[None, :]
        weight_piece = weight_piece + jnp.where(picks == hidden + at, line, 0.0)
    weights = lax.all_gather(z_swap(weight_piece.astype(BF)), ("y", "core"), axis=0, tiled=True)
    far_first, far_second = weights[:HALF], weights[HALF:]
    far_shift = jnp.sum(far_first[hidden : hidden + 3, :HALF].astype(F32), 0)

    text_units, text_norms = unit_rows(raw_caption_embedding[0].astype(F32))
    own_text = text_units.astype(BF)
    rows = own_text.shape[0]

    far = far_forward(own_text)
    one = ring_shift(own_text, 1)
    two = ring_shift(own_text, 2)
    three = ring_shift(own_text, 3)
    same = jnp.concatenate([one, two, three], 0)
    other = core_swap(same)

    raw_image = raw_image_embedding[0]
    image_units, _ = unit_rows(raw_image)
    image_bf = image_units.astype(BF)

    features = aggregated_picture_vectors[0].reshape(4, 2, rows, -1)
    features = lax.dynamic_index_in_dim(features, zh, 1, keepdims=False).reshape(4 * rows, -1).astype(F32)
    centred = features - jnp.mean(features, axis=-1, keepdims=True)
    inv_std = lax.rsqrt(jnp.mean(centred * centred, axis=-1, keepdims=True) + EPSILON)
    normalized = centred * inv_std
    layer_in = (normalized * standardize_factor + standardize_shift).astype(BF)
    near_slope = gelu_slope(
        jnp.dot(layer_in, hidden_projection_matrix, preferred_element_type=F32) + hidden_shift_vector
    )
    image_bf, near_slope = lax.optimization_barrier((image_bf, near_slope))

    texts = jnp.concatenate([own_text, far, same, other], 0)
    logits = scale * dot_nt(image_bf, texts) + shift
    columns = jnp.arange(texts.shape[0], dtype=jnp.int32)
    ids = jnp.where(columns < rows, (x * 2 + zh) * rows + columns, -1)
    match = matching_caption_slot[0][:, None] == ids[None, :]
    chance = jax.nn.sigmoid(jnp.where(match, -logits, logits))
    pair_grad = jnp.where(match, -chance, chance).astype(BF)
    image_part = (scale * jnp.dot(pair_grad, texts, preferred_element_type=F32)).astype(BF)

    by_x = lax.all_to_all(image_part, "x", 0, 0, tiled=True)
    text_parts = (scale * dot_tn(pair_grad, image_bf)).astype(BF)
    by_x, text_parts = lax.optimization_barrier((by_x, text_parts))
    sums = jnp.sum(by_x.reshape(4, 2, rows, -1).astype(F32), 0)
    kept = lax.dynamic_index_in_dim(sums, zh, 0, keepdims=False)
    sent = lax.dynamic_index_in_dim(sums, 1 - zh, 0, keepdims=False).astype(BF)
    came = z_swap(sent)

    own_part, far_part = text_parts[:rows], text_parts[rows : 2 * rows]
    same_part, other_part = text_parts[2 * rows : 5 * rows], text_parts[5 * rows :]
    met = (same_part.astype(F32) + core_swap(other_part).astype(F32)).astype(BF)
    kept, met = lax.optimization_barrier((kept, met))

    image_grad = kept + came.astype(F32)
    own_units, own_norms = unit_rows(rows_of(raw_image, (x * 2 + zh) * rows, rows))
    upstream = norm_back(image_grad, own_units, own_norms)
    upstream_bf = lax.all_to_all(
        jnp.broadcast_to(upstream.astype(BF)[None], (4,) + upstream.shape), "x", 0, 0, tiled=True
    ).reshape(4 * rows, -1)
    far_slope = gelu_slope(dot_nt(layer_in, far_first) + far_shift)
    upstream_bf, far_slope = lax.optimization_barrier((upstream_bf, far_slope))

    near_act = (dot_nt(upstream_bf, return_projection_matrix) * near_slope).astype(BF)
    far_act = (dot_nt(upstream_bf, far_second) * far_slope).astype(BF)
    back_norm = dot_nt(near_act, hidden_projection_matrix) + jnp.dot(far_act, far_first, preferred_element_type=F32)
    back_norm = back_norm * standardize_factor
    first_mean = jnp.mean(back_norm, axis=-1, keepdims=True)
    second_mean = jnp.mean(back_norm * normalized, axis=-1, keepdims=True)
    ln_part = ((back_norm - first_mean - normalized * second_mean) * inv_std).astype(BF)
    parts_x = lax.all_to_all(ln_part, "x", 0, 0, tiled=True)
    d_pooled = upstream + jnp.sum(parts_x.reshape(4, rows, -1).astype(F32), 0)

    text_grad = (
        own_part.astype(F32)
        + far_back(far_part).astype(F32)
        + ring_shift(met[:rows], -1).astype(F32)
        + ring_shift(met[rows : 2 * rows], -2).astype(F32)
        + ring_shift(met[2 * rows :], -3).astype(F32)
    )
    d_text = norm_back(text_grad, text_units, text_norms).astype(BF)
    return (d_pooled.astype(BF)[None], d_text[None])


def solution(mesh):
    fine = Mesh(mesh.devices.reshape([size for _, size in AXES]), [name for name, _ in AXES])
    placed = (
        P(OUTER, None, None),
        P(OUTER, None, None),
        P(OUTER, INNER, None),
        P(OUTER, None),
        P(),
        P(),
        P(None, INNER),
        P(INNER),
        P(INNER, None),
        P(),
        P(),
    )
    return jax.shard_map(
        local,
        mesh=fine,
        in_specs=placed,
        out_specs=(P(OUTER, INNER, None), P(OUTER, INNER, None)),
        check_vma=False,
    )
```

```python
import jax
import jax.numpy as jnp
from jax import lax
from jax.experimental import pallas as pl
from jax.experimental.pallas import tpu as pltpu
from jax.sharding import Mesh
from jax.sharding import PartitionSpec as P

SQRT_TWO_PI = 0.7978845608028654
CUBIC = 0.044715
EPSILON = 1e-06

AXES = (("x", 4), ("zh", 2), ("zl", 8), ("y", 8), ("core", 2))
SIZE = dict(AXES)
INNER = ("x", "zh")
OUTER = ("zl", "y", "core")
RING = ("zh", "zl", "y")
TXT = 48
PIECE = 72
HALF = 8 * PIECE
BF = jnp.bfloat16
F32 = jnp.float32


def permute(value, axes, target):
    count = 1
    for axis in axes:
        count *= SIZE[axis]
    return lax.ppermute(value, axes, [(source, target(source) % count) for source in range(count)])


def ring_shift(value, steps):
    return permute(value, RING, lambda at: at + steps)


def core_swap(value):
    return permute(value, ("core",), lambda at: 1 - at)


def z_swap(value):
    return permute(value, ("zh",), lambda at: 1 - at)


def z_mirror(value):
    return permute(value, ("zh", "zl"), lambda at: 15 - at)


def far_forward(value):
    return permute(value, RING + ("core",), lambda at: at + 1 if at % 2 == 0 else at + 7)


def far_back(value):
    return permute(value, RING + ("core",), lambda at: at - 1 if at % 2 == 1 else at - 7)


def dot_nt(a, b):
    return lax.dot_general(a, b, (((1,), (1,)), ((), ())), preferred_element_type=F32)


def dot_tn(a, b):
    return lax.dot_general(a, b, (((0,), (0,)), ((), ())), preferred_element_type=F32)


def gelu_slope(pre_values):
    tangent = jnp.tanh(SQRT_TWO_PI * (pre_values + CUBIC * pre_values**3))
    return 0.5 * (1.0 + tangent) + 0.5 * pre_values * (1.0 - tangent * tangent) * SQRT_TWO_PI * (
        1.0 + 3.0 * CUBIC * pre_values * pre_values
    )


def unit_rows(row_block):
    row_norms = jnp.sqrt(jnp.sum(row_block * row_block, axis=-1, keepdims=True))
    return (row_block / row_norms, row_norms)


def norm_back(grad, units, norms):
    return (grad - units * jnp.sum(units * grad, axis=-1, keepdims=True)) / norms


def rows_of(value, start, count):
    return lax.dynamic_slice_in_dim(value, start, count, 0)


def after(value, *others):
    return lax.optimization_barrier((value,) + others)[0]


def pair_rows(scale, shift, base, images, slots, blocks, texts):
    for at, block in enumerate(blocks):
        texts[TXT * at : TXT * (at + 1), :] = block[...]
    logits = scale[0] * dot_nt(images[...], texts[...]) + shift[0]
    columns = lax.broadcasted_iota(jnp.int32, logits.shape, 1)
    match = (columns < TXT) & (slots[...] == columns + base[0])
    chance = jax.nn.sigmoid(jnp.where(match, -logits, logits))
    pair_grad = jnp.where(match, -chance, chance).astype(BF)
    part = scale[0] * jnp.dot(pair_grad, texts[...], preferred_element_type=F32)
    return pair_grad, part.astype(BF)


def first_pairs(scale, shift, base, images, slots, *refs):
    blocks, (part, pair_grad, texts) = refs[:8], refs[8:]
    pair_grad[...], part[...] = pair_rows(scale, shift, base, images, slots, blocks, texts)


def second_pairs(scale, shift, base, images, slots, *refs):
    blocks, (first_grad, first_images, part, own, far, same, other, texts) = refs[:8], refs[8:]
    pair_grad, part[...] = pair_rows(scale, shift, base, images, slots, blocks, texts)
    total = scale[0] * (dot_tn(first_grad[...], first_images[...]) + dot_tn(pair_grad, images[...]))
    own[...] = total[:TXT].astype(BF)
    far[...] = total[TXT : 2 * TXT].astype(BF)
    same[...] = total[2 * TXT : 5 * TXT].astype(BF)
    other[...] = total[5 * TXT :].astype(BF)


def pair_call(kernel, outs, flops, *operands):
    scalar = pl.BlockSpec(memory_space=pltpu.SMEM)
    whole = pl.BlockSpec(memory_space=pltpu.VMEM)
    width = operands[3].shape[1]
    return pl.pallas_call(
        kernel,
        out_shape=[jax.ShapeDtypeStruct(shape, BF) for shape in outs],
        in_specs=[scalar] * 3 + [whole] * (len(operands) - 3),
        out_specs=[whole] * len(outs),
        scratch_shapes=[pltpu.VMEM((8 * TXT, width), BF)],
        compiler_params=pltpu.CompilerParams(vmem_limit_bytes=32 * 1024 * 1024),
        cost_estimate=pl.CostEstimate(flops=flops, bytes_accessed=3 * 1024 * 1024, transcendentals=192 * 384),
    )(*operands)


def local(
    aggregated_picture_vectors,
    raw_image_embedding,
    raw_caption_embedding,
    matching_caption_slot,
    standardize_factor,
    standardize_shift,
    hidden_projection_matrix,
    hidden_shift_vector,
    return_projection_matrix,
    sharpness_factor,
    similarity_shift,
):
    x = lax.axis_index("x")
    zh = lax.axis_index("zh")
    piece = lax.axis_index("y") * 2 + lax.axis_index("core")
    hidden = hidden_shift_vector.shape[0]

    picks = jnp.arange(PIECE, dtype=jnp.int32)[:, None] + piece * PIECE
    units_at = jnp.arange(hidden, dtype=jnp.int32)[None, :]
    weight_piece = dot_nt((picks == units_at).astype(BF), hidden_projection_matrix) + jnp.dot(
        (picks - HALF == units_at).astype(BF), return_projection_matrix, preferred_element_type=F32
    )
    high = lax.reduce_precision(hidden_shift_vector, 8, 7)
    middle = lax.reduce_precision(hidden_shift_vector - high, 8, 7)
    low = hidden_shift_vector - high - middle
    for at, term in enumerate((high, middle, low)):
        line = jnp.pad(term, (0, weight_piece.shape[1] - hidden))[None, :]
        weight_piece = weight_piece + jnp.where(picks == hidden + at, line, 0.0)
    weight_piece = z_mirror(weight_piece.astype(BF))

    text_units, text_norms = unit_rows(raw_caption_embedding[0].astype(F32))
    own_text = text_units.astype(BF)
    rows = own_text.shape[0]

    far = far_forward(own_text)
    three = ring_shift(own_text, 3)
    two = ring_shift(own_text, 2)
    one = ring_shift(own_text, 1)
    blocks = (own_text, far, one, two, three, core_swap(one), core_swap(two), core_swap(three))

    raw_image = raw_image_embedding[0]
    width = raw_image.shape[1]

    def half_rows(value, half):
        halves = value.reshape((4, 2, rows) + value.shape[1:])
        return lax.dynamic_index_in_dim(halves, half, 1, keepdims=False).reshape((4 * rows,) + value.shape[1:])

    away_bf = unit_rows(half_rows(raw_image, 1 - zh))[0].astype(BF)
    near_bf = unit_rows(half_rows(raw_image, zh))[0].astype(BF)
    slots = matching_caption_slot[0][:, None]
    away_slots, near_slots = half_rows(slots, 1 - zh), half_rows(slots, zh)

    features = half_rows(aggregated_picture_vectors[0], zh).astype(F32)
    centred = features - jnp.mean(features, axis=-1, keepdims=True)
    inv_std = lax.rsqrt(jnp.mean(centred * centred, axis=-1, keepdims=True) + EPSILON)
    normalized = centred * inv_std
    layer_in = (normalized * standardize_factor + standardize_shift).astype(BF)
    near_slope = gelu_slope(
        jnp.dot(layer_in, hidden_projection_matrix, preferred_element_type=F32) + hidden_shift_vector
    )
    away_bf, near_bf, near_slope, normalized = lax.optimization_barrier((away_bf, near_bf, near_slope, normalized))

    base = ((x * 2 + zh) * rows).astype(jnp.int32)[None]
    scalars = (sharpness_factor, similarity_shift, base)
    half_shape, pair_shape = (4 * rows, width), (4 * rows, 8 * rows)
    pair_flops = 4 * pair_shape[0] * pair_shape[1] * width
    away_part, away_grad = pair_call(
        first_pairs, (half_shape, pair_shape), pair_flops, *scalars, away_bf, away_slots, *blocks
    )
    away_sum = lax.all_to_all(away_part, "x", 0, 0, tiled=True)
    near_part, own_part, far_part, same_part, other_part = pair_call(
        second_pairs,
        (half_shape, (rows, width), (rows, width), (3 * rows, width), (3 * rows, width)),
        2 * pair_flops,
        *scalars,
        near_bf,
        near_slots,
        *blocks,
        away_grad,
        after(away_bf, away_part),
    )
    sent = jnp.sum(away_sum.reshape(4, rows, -1).astype(F32), 0).astype(BF)
    came = z_swap(sent)
    near_part = after(near_part, sent)
    near_sum = lax.all_to_all(near_part, "x", 0, 0, tiled=True)
    kept = jnp.sum(near_sum.reshape(4, rows, -1).astype(F32), 0)

    weights = lax.all_gather(after(weight_piece, away_part), ("y", "core"), axis=0, tiled=True)
    far_first, far_second = weights[:HALF], weights[HALF:]
    far_shift = jnp.sum(far_first[hidden : hidden + 3, :HALF].astype(F32), 0)

    met = (same_part.astype(F32) + core_swap(after(other_part, sent)).astype(F32)).astype(BF)
    far_came = far_back(after(far_part, sent))
    kept, met = lax.optimization_barrier((kept, met))

    image_grad = kept + came.astype(F32)
    own_units, own_norms = unit_rows(rows_of(raw_image, (x * 2 + zh) * rows, rows))
    upstream = norm_back(image_grad, own_units, own_norms)
    upstream_bf = lax.all_to_all(
        jnp.broadcast_to(upstream.astype(BF)[None], (4,) + upstream.shape), "x", 0, 0, tiled=True
    ).reshape(4 * rows, -1)
    far_slope = gelu_slope(dot_nt(layer_in, far_first) + far_shift)
    upstream_bf, far_slope = lax.optimization_barrier((upstream_bf, far_slope))

    near_act = (dot_nt(upstream_bf, return_projection_matrix) * near_slope).astype(BF)
    far_act = (dot_nt(upstream_bf, far_second) * far_slope).astype(BF)
    back_norm = dot_nt(near_act, hidden_projection_matrix) + jnp.dot(far_act, far_first, preferred_element_type=F32)
    back_norm = back_norm * standardize_factor
    first_mean = jnp.mean(back_norm, axis=-1, keepdims=True)
    second_mean = jnp.mean(back_norm * normalized, axis=-1, keepdims=True)
    ln_part = ((back_norm - first_mean - normalized * second_mean) * inv_std).astype(BF)
    parts_x = lax.all_to_all(ln_part, "x", 0, 0, tiled=True)
    d_pooled = upstream + jnp.sum(parts_x.reshape(4, rows, -1).astype(F32), 0)

    text_grad = (
        own_part.astype(F32)
        + far_came.astype(F32)
        + ring_shift(met[:rows], -1).astype(F32)
        + ring_shift(met[rows : 2 * rows], -2).astype(F32)
        + ring_shift(met[2 * rows :], -3).astype(F32)
    )
    d_text = norm_back(text_grad, text_units, text_norms).astype(BF)
    return (d_pooled.astype(BF)[None], d_text[None])


def solution(mesh):
    fine = Mesh(mesh.devices.reshape([size for _, size in AXES]), [name for name, _ in AXES])
    placed = (
        P(OUTER, None, None),
        P(OUTER, None, None),
        P(OUTER, INNER, None),
        P(OUTER, None),
        P(),
        P(),
        P(None, INNER),
        P(INNER),
        P(INNER, None),
        P(),
        P(),
    )
    return jax.shard_map(
        local,
        mesh=fine,
        in_specs=placed,
        out_specs=(P(OUTER, INNER, None), P(OUTER, INNER, None)),
        check_vma=False,
    )
```

```python
import jax
import jax.numpy as jnp
from jax import lax
from jax.experimental import pallas as pl
from jax.experimental.pallas import tpu as pltpu
from jax.sharding import Mesh
from jax.sharding import PartitionSpec as P

SQRT_TWO_PI = 0.7978845608028654
CUBIC = 0.044715
EPSILON = 1e-06

AXES = (("x", 4), ("zh", 2), ("zl", 8), ("y", 8), ("core", 2))
SIZE = dict(AXES)
INNER = ("x", "zh")
OUTER = ("zl", "y", "core")
RING = ("zh", "zl", "y")
TXT = 48
PIECE = 72
HALF = 8 * PIECE
BF = jnp.bfloat16
F32 = jnp.float32


def permute(value, axes, target):
    count = 1
    for axis in axes:
        count *= SIZE[axis]
    return lax.ppermute(value, axes, [(source, target(source) % count) for source in range(count)])


def ring_shift(value, steps):
    return permute(value, RING, lambda at: at + steps)


def core_swap(value):
    return permute(value, ("core",), lambda at: 1 - at)


def z_swap(value):
    return permute(value, ("zh",), lambda at: 1 - at)


def z_mirror(value):
    return permute(value, ("zh", "zl"), lambda at: 15 - at)


def far_forward(value):
    return permute(value, RING + ("core",), lambda at: at + 1 if at % 2 == 0 else at + 7)


def outer_back(value):
    return permute(value, RING + ("core",), lambda at: at - 1)


def dot_nt(a, b):
    return lax.dot_general(a, b, (((1,), (1,)), ((), ())), preferred_element_type=F32)


def dot_tn(a, b):
    return lax.dot_general(a, b, (((0,), (0,)), ((), ())), preferred_element_type=F32)


def gelu_slope(pre_values):
    tangent = jnp.tanh(SQRT_TWO_PI * (pre_values + CUBIC * pre_values**3))
    return 0.5 * (1.0 + tangent) + 0.5 * pre_values * (1.0 - tangent * tangent) * SQRT_TWO_PI * (
        1.0 + 3.0 * CUBIC * pre_values * pre_values
    )


def unit_rows(row_block):
    row_norms = jnp.sqrt(jnp.sum(row_block * row_block, axis=-1, keepdims=True))
    return (row_block / row_norms, row_norms)


def norm_back(grad, units, norms):
    return (grad - units * jnp.sum(units * grad, axis=-1, keepdims=True)) / norms


def rows_of(value, start, count):
    return lax.dynamic_slice_in_dim(value, start, count, 0)


def after(value, *others):
    return lax.optimization_barrier((value,) + others)[0]


def pair_rows(scale, shift, base, images, slots, blocks, texts):
    for at, block in enumerate(blocks):
        texts[TXT * at : TXT * (at + 1), :] = block[...]
    logits = scale[0] * dot_nt(images[...], texts[...]) + shift[0]
    columns = lax.broadcasted_iota(jnp.int32, logits.shape, 1)
    match = (columns < TXT) & (slots[...] == columns + base[0])
    chance = jax.nn.sigmoid(jnp.where(match, -logits, logits))
    pair_grad = jnp.where(match, -chance, chance).astype(BF)
    part = scale[0] * jnp.dot(pair_grad, texts[...], preferred_element_type=F32)
    return pair_grad, part.astype(BF)


def first_pairs(scale, shift, base, images, slots, *refs):
    blocks, (part, pair_grad, texts) = refs[:8], refs[8:]
    pair_grad[...], part[...] = pair_rows(scale, shift, base, images, slots, blocks, texts)


def second_pairs(scale, shift, base, images, slots, *refs):
    blocks, (first_grad, first_images, part, even, odd, texts) = refs[:8], refs[8:]
    pair_grad, part[...] = pair_rows(scale, shift, base, images, slots, blocks, texts)
    total = scale[0] * (dot_tn(first_grad[...], first_images[...]) + dot_tn(pair_grad, images[...]))
    even[...] = total[: 4 * TXT].astype(BF)
    far, swap_two, swap_one, swap_three = (total[TXT * at : TXT * (at + 1)] for at in range(4, 8))
    on_one = base[1] == 1
    odd[:TXT] = jnp.where(on_one, far, swap_one).astype(BF)
    odd[TXT : 2 * TXT] = jnp.where(on_one, swap_two, swap_three).astype(BF)
    odd[2 * TXT : 3 * TXT] = jnp.where(on_one, swap_one, swap_two).astype(BF)
    odd[3 * TXT :] = jnp.where(on_one, swap_three, far).astype(BF)


def upstream_rows(sums, came, raw, upstream, spread):
    grad = came[...].astype(F32)
    for at in range(4):
        grad = grad + sums[TXT * at : TXT * (at + 1), :].astype(F32)
    units, norms = unit_rows(raw[...])
    rows = norm_back(grad, units, norms)
    upstream[...] = rows
    for at in range(4):
        spread[TXT * at : TXT * (at + 1), :] = rows.astype(BF)


def mlp_back(up, near_slope, near_second, near_first, far_slope, far_weights, factor, normalized, inv_std, out):
    near_act = (dot_nt(up[...], near_second[...]) * near_slope[...]).astype(BF)
    far_act = (dot_nt(up[...], far_weights[HALF:, :]) * far_slope[...]).astype(BF)
    back = jnp.dot(far_act, far_weights[:HALF, :], preferred_element_type=F32)
    back = (back + dot_nt(near_act, near_first[...])) * factor[...]
    first_mean = jnp.mean(back, axis=-1, keepdims=True)
    second_mean = jnp.mean(back * normalized[...], axis=-1, keepdims=True)
    out[...] = ((back - first_mean - normalized[...] * second_mean) * inv_std[...]).astype(BF)


def whole_call(kernel, outs, flops, *operands):
    whole = pl.BlockSpec(memory_space=pltpu.VMEM)
    return pl.pallas_call(
        kernel,
        out_shape=outs,
        in_specs=[whole] * len(operands),
        out_specs=[whole] * len(outs),
        compiler_params=pltpu.CompilerParams(vmem_limit_bytes=40 * 1024 * 1024),
        cost_estimate=pl.CostEstimate(flops=flops, bytes_accessed=1024 * 1024, transcendentals=0),
    )(*operands)


def pair_call(kernel, outs, flops, *operands):
    scalar = pl.BlockSpec(memory_space=pltpu.SMEM)
    whole = pl.BlockSpec(memory_space=pltpu.VMEM)
    width = operands[3].shape[1]
    return pl.pallas_call(
        kernel,
        out_shape=[jax.ShapeDtypeStruct(shape, BF) for shape in outs],
        in_specs=[scalar] * 3 + [whole] * (len(operands) - 3),
        out_specs=[whole] * len(outs),
        scratch_shapes=[pltpu.VMEM((8 * TXT, width), BF)],
        compiler_params=pltpu.CompilerParams(vmem_limit_bytes=32 * 1024 * 1024),
        cost_estimate=pl.CostEstimate(flops=flops, bytes_accessed=3 * 1024 * 1024, transcendentals=192 * 384),
    )(*operands)


def local(
    aggregated_picture_vectors,
    raw_image_embedding,
    raw_caption_embedding,
    matching_caption_slot,
    standardize_factor,
    standardize_shift,
    hidden_projection_matrix,
    hidden_shift_vector,
    return_projection_matrix,
    sharpness_factor,
    similarity_shift,
):
    x = lax.axis_index("x")
    zh = lax.axis_index("zh")
    piece = lax.axis_index("y") * 2 + lax.axis_index("core")
    hidden = hidden_shift_vector.shape[0]

    picks = jnp.arange(PIECE, dtype=jnp.int32)[:, None] + piece * PIECE
    units_at = jnp.arange(hidden, dtype=jnp.int32)[None, :]
    weight_piece = dot_nt((picks == units_at).astype(BF), hidden_projection_matrix) + jnp.dot(
        (picks - HALF == units_at).astype(BF), return_projection_matrix, preferred_element_type=F32
    )
    high = lax.reduce_precision(hidden_shift_vector, 8, 7)
    middle = lax.reduce_precision(hidden_shift_vector - high, 8, 7)
    low = hidden_shift_vector - high - middle
    for at, term in enumerate((high, middle, low)):
        line = jnp.pad(term, (0, weight_piece.shape[1] - hidden))[None, :]
        weight_piece = weight_piece + jnp.where(picks == hidden + at, line, 0.0)
    weight_sent = weight_piece.astype(BF)
    weight_piece = z_mirror(weight_sent)

    text_units, text_norms = unit_rows(raw_caption_embedding[0].astype(F32))
    own_text = text_units.astype(BF)
    rows = own_text.shape[0]

    own_text = after(own_text, weight_sent)
    far = far_forward(own_text)
    three = ring_shift(own_text, 3)
    two = ring_shift(own_text, 2)
    one = ring_shift(own_text, 1)

    raw_image = after(raw_image_embedding[0], own_text)
    width = raw_image.shape[1]

    def half_rows(value, half):
        halves = value.reshape((4, 2, rows) + value.shape[1:])
        return lax.dynamic_index_in_dim(halves, half, 1, keepdims=False).reshape((4 * rows,) + value.shape[1:])

    away_bf = unit_rows(half_rows(raw_image, 1 - zh))[0].astype(BF)
    near_bf = unit_rows(half_rows(raw_image, zh))[0].astype(BF)
    slots = matching_caption_slot[0][:, None]
    away_slots, near_slots = half_rows(slots, 1 - zh), half_rows(slots, zh)

    swaps = tuple(core_swap(after(block, away_bf, near_bf, away_slots, near_slots)) for block in (two, one, three))
    blocks = (own_text, two, one, three, far) + swaps
    weights = lax.all_gather(after(weight_piece, far, *swaps), ("y", "core"), axis=0, tiled=True)
    away_bf, near_bf, away_slots, near_slots = lax.optimization_barrier((away_bf, near_bf, away_slots, near_slots))

    base = jnp.stack([(x * 2 + zh) * rows, lax.axis_index("core")]).astype(jnp.int32)
    scalars = (sharpness_factor, similarity_shift, base)
    half_shape, pair_shape = (4 * rows, width), (4 * rows, 8 * rows)
    pair_flops = 4 * pair_shape[0] * pair_shape[1] * width
    away_part, away_grad = pair_call(
        first_pairs, (half_shape, pair_shape), pair_flops, *scalars, away_bf, away_slots, *blocks
    )
    away_sum = lax.all_to_all(away_part, "x", 0, 0, tiled=True)
    near_part, even_part, odd_part = pair_call(
        second_pairs,
        (half_shape, half_shape, half_shape),
        2 * pair_flops,
        *scalars,
        near_bf,
        near_slots,
        *blocks,
        away_grad,
        after(away_bf, away_part),
    )
    near_sum = lax.all_to_all(near_part, "x", 0, 0, tiled=True)
    sent = jnp.sum(after(away_sum, near_part).reshape(4, rows, -1).astype(F32), 0).astype(BF)
    came = z_swap(sent)

    features = after(half_rows(aggregated_picture_vectors[0], zh), sent).astype(F32)
    centred = features - jnp.mean(features, axis=-1, keepdims=True)
    inv_std = lax.rsqrt(jnp.mean(centred * centred, axis=-1, keepdims=True) + EPSILON)
    normalized = centred * inv_std
    layer_in = (normalized * standardize_factor + standardize_shift).astype(BF)
    near_slope = gelu_slope(
        jnp.dot(layer_in, hidden_projection_matrix, preferred_element_type=F32) + hidden_shift_vector
    )

    met = even_part.astype(F32) + outer_back(after(odd_part, sent)).astype(F32)
    met_sent = met[2 * rows :].astype(BF)
    came, normalized, near_slope, met_sent = lax.optimization_barrier((came, normalized, near_slope, met_sent))

    own_raw = rows_of(raw_image, (x * 2 + zh) * rows, rows)
    upstream, spread = whole_call(
        upstream_rows,
        [jax.ShapeDtypeStruct((rows, width), F32), jax.ShapeDtypeStruct(half_shape, BF)],
        1024 * 1024,
        near_sum,
        came,
        own_raw,
    )
    upstream_bf = lax.all_to_all(spread, "x", 0, 0, tiled=True)

    far_first = weights[:HALF]
    far_shift = jnp.sum(far_first[hidden : hidden + 3, :HALF].astype(F32), 0)
    far_slope = gelu_slope(dot_nt(after(layer_in, spread), far_first) + far_shift)
    pair_met = met[: 2 * rows] + ring_shift(after(met_sent, far_slope), -1).astype(F32)
    (ln_part,) = whole_call(
        mlp_back,
        [jax.ShapeDtypeStruct(half_shape, BF)],
        8 * 4 * rows * HALF * width,
        upstream_bf,
        near_slope,
        return_projection_matrix,
        hidden_projection_matrix,
        far_slope,
        weights,
        standardize_factor[None, :],
        normalized,
        inv_std,
    )
    parts_x = lax.all_to_all(ln_part, "x", 0, 0, tiled=True)
    d_pooled = upstream + jnp.sum(parts_x.reshape(4, rows, -1).astype(F32), 0)

    text_grad = pair_met[:rows] + ring_shift(pair_met[rows:].astype(BF), -2).astype(F32)
    d_text = norm_back(text_grad, text_units, text_norms).astype(BF)
    return (d_pooled.astype(BF)[None], d_text[None])


def solution(mesh):
    fine = Mesh(mesh.devices.reshape([size for _, size in AXES]), [name for name, _ in AXES])
    placed = (
        P(OUTER, None, None),
        P(OUTER, None, None),
        P(OUTER, INNER, None),
        P(OUTER, None),
        P(),
        P(),
        P(None, INNER),
        P(INNER),
        P(INNER, None),
        P(),
        P(),
    )
    return jax.shard_map(
        local,
        mesh=fine,
        in_specs=placed,
        out_specs=(P(OUTER, INNER, None), P(OUTER, INNER, None)),
        check_vma=False,
    )
```

```python
import jax
import jax.numpy as jnp
from jax import lax
from jax.experimental import pallas as pl
from jax.experimental.pallas import tpu as pltpu
from jax.sharding import Mesh
from jax.sharding import PartitionSpec as P

SQRT_TWO_PI = 0.7978845608028654
CUBIC = 0.044715
EPSILON = 1e-06

AXES = (("x", 4), ("zh", 2), ("zl", 8), ("y", 8), ("core", 2))
SIZE = dict(AXES)
INNER = ("x", "zh")
OUTER = ("zl", "y", "core")
RING = ("zh", "zl", "y")
TXT = 48
PIECE = 72
HALF = 8 * PIECE
BF = jnp.bfloat16
F32 = jnp.float32


def permute(value, axes, target):
    count = 1
    for axis in axes:
        count *= SIZE[axis]
    return lax.ppermute(value, axes, [(source, target(source) % count) for source in range(count)])


def ring_shift(value, steps):
    return permute(value, RING, lambda at: at + steps)


def core_swap(value):
    return permute(value, ("core",), lambda at: 1 - at)


def z_swap(value):
    return permute(value, ("zh",), lambda at: 1 - at)


def z_mirror(value):
    return permute(value, ("zh", "zl"), lambda at: 15 - at)


def far_forward(value):
    return permute(value, RING + ("core",), lambda at: at + 1 if at % 2 == 0 else at + 7)


def outer_back(value):
    return permute(value, RING + ("core",), lambda at: at - 1)


def dot_nt(a, b):
    return lax.dot_general(a, b, (((1,), (1,)), ((), ())), preferred_element_type=F32)


def dot_tn(a, b):
    return lax.dot_general(a, b, (((0,), (0,)), ((), ())), preferred_element_type=F32)


def gelu_slope(pre_values):
    tangent = jnp.tanh(SQRT_TWO_PI * (pre_values + CUBIC * pre_values**3))
    return 0.5 * (1.0 + tangent) + 0.5 * pre_values * (1.0 - tangent * tangent) * SQRT_TWO_PI * (
        1.0 + 3.0 * CUBIC * pre_values * pre_values
    )


def unit_rows(row_block):
    row_norms = jnp.sqrt(jnp.sum(row_block * row_block, axis=-1, keepdims=True))
    return (row_block / row_norms, row_norms)


def norm_back(grad, units, norms):
    return (grad - units * jnp.sum(units * grad, axis=-1, keepdims=True)) / norms


def rows_of(value, start, count):
    return lax.dynamic_slice_in_dim(value, start, count, 0)


def after(value, *others):
    return lax.optimization_barrier((value,) + others)[0]


def pair_grads(scale, shift, base, images, slots, texts):
    logits = scale[0] * dot_nt(images[...], texts[...]) + shift[0]
    columns = lax.broadcasted_iota(jnp.int32, logits.shape, 1)
    match = (columns < TXT) & (slots[...] == columns + base[0])
    chance = jax.nn.sigmoid(jnp.where(match, -logits, logits))
    return jnp.where(match, -chance, chance).astype(BF)


def side_by_side(blocks, texts):
    for at, block in enumerate(blocks):
        texts[TXT * at : TXT * (at + 1), :] = block[...]


def first_pairs(scale, shift, base, images, slots, *refs):
    blocks, (part, texts) = refs[:8], refs[8:]
    side_by_side(blocks, texts)
    pair_grad = pair_grads(scale, shift, base, images, slots, texts)
    part[...] = (scale[0] * jnp.dot(pair_grad, texts[...], preferred_element_type=F32)).astype(BF)


def second_pairs(scale, shift, base, images, slots, *refs):
    blocks, (first_images, first_slots, part, even, odd, texts) = refs[:8], refs[8:]
    side_by_side(blocks, texts)
    pair_grad = pair_grads(scale, shift, base, images, slots, texts)
    part[...] = (scale[0] * jnp.dot(pair_grad, texts[...], preferred_element_type=F32)).astype(BF)
    first_grad = pair_grads(scale, shift, base, first_images, first_slots, texts)
    total = scale[0] * (dot_tn(first_grad, first_images[...]) + dot_tn(pair_grad, images[...]))
    even[...] = total[: 4 * TXT].astype(BF)
    far, swap_two, swap_one, swap_three = (total[TXT * at : TXT * (at + 1)] for at in range(4, 8))
    on_one = base[1] == 1
    odd[:TXT] = jnp.where(on_one, far, swap_one).astype(BF)
    odd[TXT : 2 * TXT] = jnp.where(on_one, swap_two, swap_three).astype(BF)
    odd[2 * TXT : 3 * TXT] = jnp.where(on_one, swap_one, swap_two).astype(BF)
    odd[3 * TXT :] = jnp.where(on_one, swap_three, far).astype(BF)


def upstream_rows(sums, came, raw, upstream, spread):
    grad = came[...].astype(F32)
    for at in range(4):
        grad = grad + sums[TXT * at : TXT * (at + 1), :].astype(F32)
    units, norms = unit_rows(raw[...])
    rows = norm_back(grad, units, norms)
    upstream[...] = rows
    for at in range(4):
        spread[TXT * at : TXT * (at + 1), :] = rows.astype(BF)


def text_rows(raw, out):
    out[...] = unit_rows(raw[...].astype(F32))[0].astype(BF)


def piece_rows(at, first, second, shift, out):
    hidden, start = first.shape[0], at[0] * PIECE
    picks = lax.broadcasted_iota(jnp.int32, (PIECE, hidden), 0) + start
    units_at = lax.broadcasted_iota(jnp.int32, (PIECE, hidden), 1)
    value = jnp.dot(
        jnp.where(picks == units_at, 1.0, 0.0).astype(BF), first[...], preferred_element_type=F32
    ) + jnp.dot(jnp.where(picks - HALF == units_at, 1.0, 0.0).astype(BF), second[...], preferred_element_type=F32)
    rows = lax.broadcasted_iota(jnp.int32, value.shape, 0) + start
    left = shift[...]
    for term_at in range(3):
        term = left.astype(BF).astype(F32)
        left = left - term
        value = value + jnp.where(rows == hidden + term_at, term, 0.0)
    out[...] = value.astype(BF)


def mlp_back(factor, inv_std, *refs):
    count = 7
    sources, out, held, done = refs[:count], refs[count], refs[count + 1 : -1], refs[-1]
    up, near_second, near_slope, layer_in, far_weights, near_first, normalized = held
    copies = [pltpu.make_async_copy(a, b, done.at[at]) for at, (a, b) in enumerate(zip(sources, held))]
    for copy in copies:
        copy.start()
    hidden = near_second.shape[0]
    copies[0].wait()
    copies[1].wait()
    near_back = dot_nt(up[...], near_second[...])
    copies[2].wait()
    near_act = (near_back * near_slope[...]).astype(BF)
    copies[3].wait()
    copies[4].wait()
    low, high = hidden // 16 * 16, (hidden + 3 + 15) // 16 * 16
    spare = far_weights[low:high, :].astype(F32)
    row = lax.broadcasted_iota(jnp.int32, spare.shape, 0) + low
    shift = jnp.sum(jnp.where((row >= hidden) & (row < hidden + 3), spare, 0.0), axis=0, keepdims=True)
    far_slope = gelu_slope(dot_nt(layer_in[...], far_weights[:HALF, :]) + shift[:, :HALF])
    far_act = (dot_nt(up[...], far_weights[HALF:, :]) * far_slope).astype(BF)
    copies[5].wait()
    copies[6].wait()
    back = jnp.dot(near_act, near_first[...], preferred_element_type=F32)
    back = (back + jnp.dot(far_act, far_weights[:HALF, :], preferred_element_type=F32)) * factor[...]
    first_mean = jnp.mean(back, axis=-1, keepdims=True)
    second_mean = jnp.mean(back * normalized[...], axis=-1, keepdims=True)
    out[...] = ((back - first_mean - normalized[...] * second_mean) * inv_std[...]).astype(BF)


def whole_call(kernel, outs, flops, *operands, fetched=(), scalars=0, vmem=40):
    whole = pl.BlockSpec(memory_space=pltpu.VMEM)
    specs = [pl.BlockSpec(memory_space=pltpu.SMEM)] * scalars + [whole] * (len(operands) - scalars)
    scratch = [pltpu.VMEM(value.shape, value.dtype) for value in fetched]
    if fetched:
        scratch.append(pltpu.SemaphoreType.DMA((len(fetched),)))
    return pl.pallas_call(
        kernel,
        out_shape=outs,
        in_specs=specs + [pl.BlockSpec(memory_space=pl.ANY)] * len(fetched),
        out_specs=[whole] * len(outs),
        scratch_shapes=scratch,
        compiler_params=pltpu.CompilerParams(vmem_limit_bytes=vmem * 1024 * 1024),
        cost_estimate=pl.CostEstimate(flops=flops, bytes_accessed=1024 * 1024, transcendentals=0),
    )(*operands, *fetched)


def pair_call(kernel, outs, flops, *operands):
    scalar = pl.BlockSpec(memory_space=pltpu.SMEM)
    whole = pl.BlockSpec(memory_space=pltpu.VMEM)
    width = operands[3].shape[1]
    return pl.pallas_call(
        kernel,
        out_shape=[jax.ShapeDtypeStruct(shape, BF) for shape in outs],
        in_specs=[scalar] * 3 + [whole] * (len(operands) - 3),
        out_specs=[whole] * len(outs),
        scratch_shapes=[pltpu.VMEM((8 * TXT, width), BF)],
        compiler_params=pltpu.CompilerParams(vmem_limit_bytes=32 * 1024 * 1024),
        cost_estimate=pl.CostEstimate(flops=flops, bytes_accessed=3 * 1024 * 1024, transcendentals=192 * 384),
    )(*operands)


def local(
    aggregated_picture_vectors,
    raw_image_embedding,
    raw_caption_embedding,
    matching_caption_slot,
    standardize_factor,
    standardize_shift,
    hidden_projection_matrix,
    hidden_shift_vector,
    return_projection_matrix,
    sharpness_factor,
    similarity_shift,
):
    x = lax.axis_index("x")
    zh = lax.axis_index("zh")
    piece = lax.axis_index("y") * 2 + lax.axis_index("core")
    hidden = hidden_shift_vector.shape[0]

    raw_text = raw_caption_embedding[0]
    rows, width = raw_text.shape
    (own_text,) = whole_call(text_rows, [jax.ShapeDtypeStruct((rows, width), BF)], 1024 * 1024, raw_text)
    three = ring_shift(own_text, 3)

    near_first = hidden_projection_matrix.T
    (weight_sent,) = whole_call(
        piece_rows,
        [jax.ShapeDtypeStruct((PIECE, width), BF)],
        1024 * 1024,
        piece.astype(jnp.int32)[None],
        near_first,
        return_projection_matrix,
        jnp.pad(hidden_shift_vector, (0, width - hidden))[None, :],
        scalars=1,
    )
    weight_piece = z_mirror(weight_sent)

    own_later = after(own_text, weight_sent)
    far = far_forward(own_later)
    two = ring_shift(own_later, 2)
    one = ring_shift(own_later, 1)

    raw_image = after(raw_image_embedding[0], own_text)

    def half_rows(value, half):
        halves = value.reshape((4, 2, rows) + value.shape[1:])
        return lax.dynamic_index_in_dim(halves, half, 1, keepdims=False).reshape((4 * rows,) + value.shape[1:])

    away_bf = unit_rows(half_rows(raw_image, 1 - zh))[0].astype(BF)
    near_bf = unit_rows(half_rows(raw_image, zh))[0].astype(BF)
    slots = matching_caption_slot[0][:, None]
    away_slots, near_slots = half_rows(slots, 1 - zh), half_rows(slots, zh)

    swaps = tuple(core_swap(after(block, away_bf, near_bf, away_slots, near_slots)) for block in (two, one, three))
    blocks = (own_text, two, one, three, far) + swaps
    weights = lax.all_gather(after(weight_piece, far, *swaps), ("y", "core"), axis=0, tiled=True)
    away_bf, near_bf, away_slots, near_slots = lax.optimization_barrier((away_bf, near_bf, away_slots, near_slots))

    base = jnp.stack([(x * 2 + zh) * rows, lax.axis_index("core")]).astype(jnp.int32)
    scalars = (sharpness_factor, similarity_shift, base)
    half_shape, pair_shape = (4 * rows, width), (4 * rows, 8 * rows)
    pair_flops = 4 * pair_shape[0] * pair_shape[1] * width
    (away_part,) = pair_call(first_pairs, (half_shape,), pair_flops, *scalars, away_bf, away_slots, *blocks)
    away_sum = lax.all_to_all(away_part, "x", 0, 0, tiled=True)
    near_part, even_part, odd_part = pair_call(
        second_pairs,
        (half_shape, half_shape, half_shape),
        2 * pair_flops,
        *scalars,
        near_bf,
        near_slots,
        *blocks,
        after(away_bf, away_part),
        away_slots,
    )
    sent = jnp.sum(after(away_sum, near_part).reshape(4, rows, -1).astype(F32), 0).astype(BF)
    came = z_swap(sent)

    features = after(half_rows(aggregated_picture_vectors[0], zh), sent).astype(F32)
    centred = features - jnp.mean(features, axis=-1, keepdims=True)
    inv_std = lax.rsqrt(jnp.mean(centred * centred, axis=-1, keepdims=True) + EPSILON)
    normalized = centred * inv_std
    layer_in = (normalized * standardize_factor + standardize_shift).astype(BF)
    near_slope = gelu_slope(
        jnp.dot(layer_in, hidden_projection_matrix, preferred_element_type=F32) + hidden_shift_vector
    )

    own_raw = rows_of(raw_image, (x * 2 + zh) * rows, rows)
    near_sum = lax.all_to_all(after(near_part, layer_in, own_raw), "x", 0, 0, tiled=True)

    met = even_part.astype(F32) + outer_back(odd_part).astype(F32)
    met_sent = met[2 * rows :].astype(BF)
    came, normalized, near_slope, layer_in = lax.optimization_barrier((came, normalized, near_slope, layer_in))

    upstream, spread = whole_call(
        upstream_rows,
        [jax.ShapeDtypeStruct((rows, width), F32), jax.ShapeDtypeStruct(half_shape, BF)],
        1024 * 1024,
        near_sum,
        came,
        own_raw,
    )
    upstream_bf = lax.all_to_all(spread, "x", 0, 0, tiled=True)

    pair_met = met[: 2 * rows] + ring_shift(met_sent, -1).astype(F32)
    pair_sent = pair_met[rows:].astype(BF)
    (ln_part,) = whole_call(
        mlp_back,
        [jax.ShapeDtypeStruct(half_shape, BF)],
        8 * 4 * rows * HALF * width,
        standardize_factor[None, :],
        inv_std,
        fetched=(
            after(upstream_bf, pair_sent),
            return_projection_matrix,
            near_slope,
            layer_in,
            weights,
            near_first,
            normalized,
        ),
        vmem=58,
    )
    parts_x = lax.all_to_all(ln_part, "x", 0, 0, tiled=True)
    d_pooled = upstream + jnp.sum(parts_x.reshape(4, rows, -1).astype(F32), 0)

    text_grad = pair_met[:rows] + ring_shift(pair_sent, -2).astype(F32)
    text_units, text_norms = unit_rows(raw_text.astype(F32))
    d_text = norm_back(text_grad, text_units, text_norms).astype(BF)
    return (d_pooled.astype(BF)[None], d_text[None])


def solution(mesh):
    fine = Mesh(mesh.devices.reshape([size for _, size in AXES]), [name for name, _ in AXES])
    placed = (
        P(OUTER, None, None),
        P(OUTER, None, None),
        P(OUTER, INNER, None),
        P(OUTER, None),
        P(),
        P(),
        P(None, INNER),
        P(INNER),
        P(INNER, None),
        P(),
        P(),
    )
    return jax.shard_map(
        local,
        mesh=fine,
        in_specs=placed,
        out_specs=(P(OUTER, INNER, None), P(OUTER, INNER, None)),
        check_vma=False,
    )
```

```python
import jax
import jax.numpy as jnp
from jax import lax
from jax.experimental import pallas as pl
from jax.experimental.pallas import tpu as pltpu
from jax.sharding import Mesh
from jax.sharding import PartitionSpec as P

SQRT_TWO_PI = 0.7978845608028654
CUBIC = 0.044715
EPSILON = 1e-06

AXES = (("x", 4), ("zh", 2), ("zl", 8), ("y", 8), ("core", 2))
SIZE = dict(AXES)
INNER = ("x", "zh")
OUTER = ("zl", "y", "core")
RING = ("zh", "zl", "y")
TXT = 48
PIECE = 72
HALF = 8 * PIECE
BF = jnp.bfloat16
F32 = jnp.float32


def permute(value, axes, target):
    count = 1
    for axis in axes:
        count *= SIZE[axis]
    return lax.ppermute(value, axes, [(source, target(source) % count) for source in range(count)])


def ring_shift(value, steps):
    return permute(value, RING, lambda at: at + steps)


def z_swap(value):
    return permute(value, ("zh",), lambda at: 1 - at)


def outer_on(value):
    return permute(value, RING + ("core",), lambda at: at + 1)


def outer_back(value):
    return permute(value, RING + ("core",), lambda at: at - 1)


def dot_nt(a, b):
    return lax.dot_general(a, b, (((1,), (1,)), ((), ())), preferred_element_type=F32)


def dot_tn(a, b):
    return lax.dot_general(a, b, (((0,), (0,)), ((), ())), preferred_element_type=F32)


def gelu_slope(pre_values):
    tangent = jnp.tanh(SQRT_TWO_PI * (pre_values + CUBIC * pre_values**3))
    return 0.5 * (1.0 + tangent) + 0.5 * pre_values * (1.0 - tangent * tangent) * SQRT_TWO_PI * (
        1.0 + 3.0 * CUBIC * pre_values * pre_values
    )


def unit_rows(row_block):
    row_norms = jnp.sqrt(jnp.sum(row_block * row_block, axis=-1, keepdims=True))
    return (row_block / row_norms, row_norms)


def norm_back(grad, units, norms):
    return (grad - units * jnp.sum(units * grad, axis=-1, keepdims=True)) / norms


def rows_of(value, start, count):
    return lax.dynamic_slice_in_dim(value, start, count, 0)


def after(value, *others):
    return lax.optimization_barrier((value,) + others)[0]


def pair_grads(scale, shift, base, images, slots, texts):
    logits = scale[0] * dot_nt(images[...], texts[...]) + shift[0]
    columns = lax.broadcasted_iota(jnp.int32, logits.shape, 1)
    match = (columns < TXT) & (slots[...] == columns + base[0])
    chance = jax.nn.sigmoid(jnp.where(match, -logits, logits))
    return jnp.where(match, -chance, chance).astype(BF)


def side_by_side(first, second, out):
    split = first.shape[0]
    out[:split, :] = first[...]
    out[split:, :] = second[...]


def first_pairs(scale, shift, base, images, slots, even, odd, part, texts):
    side_by_side(even, odd, texts)
    pair_grad = pair_grads(scale, shift, base, images, slots, texts)
    part[...] = (scale[0] * jnp.dot(pair_grad, texts[...], preferred_element_type=F32)).astype(BF)


def second_pairs(scale, shift, base, images, slots, even, odd, first_images, first_slots, part, to_even, to_odd, texts):
    side_by_side(even, odd, texts)
    pair_grad = pair_grads(scale, shift, base, images, slots, texts)
    part[...] = (scale[0] * jnp.dot(pair_grad, texts[...], preferred_element_type=F32)).astype(BF)
    first_grad = pair_grads(scale, shift, base, first_images, first_slots, texts)
    total = scale[0] * (dot_tn(first_grad, first_images[...]) + dot_tn(pair_grad, images[...]))
    to_even[...] = total[: 4 * TXT].astype(BF)
    to_odd[...] = total[4 * TXT :].astype(BF)


def upstream_rows(sums, came, raw, upstream, spread):
    grad = came[...].astype(F32)
    for at in range(4):
        grad = grad + sums[TXT * at : TXT * (at + 1), :].astype(F32)
    units, norms = unit_rows(raw[...])
    rows = norm_back(grad, units, norms)
    upstream[...] = rows
    for at in range(4):
        spread[TXT * at : TXT * (at + 1), :] = rows.astype(BF)


def text_rows(raw, out):
    out[...] = unit_rows(raw[...].astype(F32))[0].astype(BF)


def piece_rows(at, first, second, shift, out):
    hidden, start = first.shape[0], at[0] * PIECE
    picks = lax.broadcasted_iota(jnp.int32, (PIECE, hidden), 0) + start
    units_at = lax.broadcasted_iota(jnp.int32, (PIECE, hidden), 1)
    value = jnp.dot(
        jnp.where(picks == units_at, 1.0, 0.0).astype(BF), first[...], preferred_element_type=F32
    ) + jnp.dot(jnp.where(picks - HALF == units_at, 1.0, 0.0).astype(BF), second[...], preferred_element_type=F32)
    rows = lax.broadcasted_iota(jnp.int32, value.shape, 0) + start
    left = shift[...]
    for term_at in range(3):
        term = left.astype(BF).astype(F32)
        left = left - term
        value = value + jnp.where(rows == hidden + term_at, term, 0.0)
    out[0] = value.astype(BF)
    out[1] = value.astype(BF)


def mlp_back(up, factor, inv_std, *refs):
    count = 6
    sources, out, held, done = refs[:count], refs[count], refs[count + 1 : -1], refs[-1]
    near_second, near_slope, layer_in, far_weights, near_first, normalized = held
    copies = [pltpu.make_async_copy(a, b, done.at[at]) for at, (a, b) in enumerate(zip(sources, held))]
    for copy in copies:
        copy.start()
    hidden = near_second.shape[0]
    copies[0].wait()
    near_back = dot_nt(up[...], near_second[...])
    copies[1].wait()
    near_act = (near_back * near_slope[...]).astype(BF)
    copies[2].wait()
    copies[3].wait()
    low, high = hidden // 16 * 16, (hidden + 3 + 15) // 16 * 16
    spare = far_weights[low:high, :].astype(F32)
    row = lax.broadcasted_iota(jnp.int32, spare.shape, 0) + low
    shift = jnp.sum(jnp.where((row >= hidden) & (row < hidden + 3), spare, 0.0), axis=0, keepdims=True)
    far_slope = gelu_slope(dot_nt(layer_in[...], far_weights[:HALF, :]) + shift[:, :HALF])
    far_act = (dot_nt(up[...], far_weights[HALF:, :]) * far_slope).astype(BF)
    copies[4].wait()
    copies[5].wait()
    back = jnp.dot(near_act, near_first[...], preferred_element_type=F32)
    back = (back + jnp.dot(far_act, far_weights[:HALF, :], preferred_element_type=F32)) * factor[...]
    first_mean = jnp.mean(back, axis=-1, keepdims=True)
    second_mean = jnp.mean(back * normalized[...], axis=-1, keepdims=True)
    out[...] = ((back - first_mean - normalized[...] * second_mean) * inv_std[...]).astype(BF)


def whole_call(kernel, outs, flops, *operands, fetched=(), scalars=0, vmem=8):
    whole = pl.BlockSpec(memory_space=pltpu.VMEM)
    specs = [pl.BlockSpec(memory_space=pltpu.SMEM)] * scalars + [whole] * (len(operands) - scalars)
    scratch = [pltpu.VMEM(value.shape, value.dtype) for value in fetched]
    if fetched:
        scratch.append(pltpu.SemaphoreType.DMA((len(fetched),)))
    return pl.pallas_call(
        kernel,
        out_shape=outs,
        in_specs=specs + [pl.BlockSpec(memory_space=pl.ANY)] * len(fetched),
        out_specs=[whole] * len(outs),
        scratch_shapes=scratch,
        compiler_params=pltpu.CompilerParams(vmem_limit_bytes=vmem * 1024 * 1024),
        cost_estimate=pl.CostEstimate(flops=flops, bytes_accessed=1024 * 1024, transcendentals=0),
    )(*operands, *fetched)


def pair_call(kernel, outs, flops, *operands):
    scalar = pl.BlockSpec(memory_space=pltpu.SMEM)
    whole = pl.BlockSpec(memory_space=pltpu.VMEM)
    width = operands[3].shape[1]
    return pl.pallas_call(
        kernel,
        out_shape=[jax.ShapeDtypeStruct(shape, BF) for shape in outs],
        in_specs=[scalar] * 3 + [whole] * (len(operands) - 3),
        out_specs=[whole] * len(outs),
        scratch_shapes=[pltpu.VMEM((8 * TXT, width), BF)],
        compiler_params=pltpu.CompilerParams(vmem_limit_bytes=20 * 1024 * 1024),
        cost_estimate=pl.CostEstimate(flops=flops, bytes_accessed=3 * 1024 * 1024, transcendentals=192 * 384),
    )(*operands)


def local(
    aggregated_picture_vectors,
    raw_image_embedding,
    raw_caption_embedding,
    matching_caption_slot,
    standardize_factor,
    standardize_shift,
    hidden_projection_matrix,
    hidden_shift_vector,
    return_projection_matrix,
    sharpness_factor,
    similarity_shift,
):
    x = lax.axis_index("x")
    zh = lax.axis_index("zh")
    piece = lax.axis_index("y") * 2 + lax.axis_index("core")
    hidden = hidden_shift_vector.shape[0]

    raw_text = raw_caption_embedding[0]
    rows, width = raw_text.shape
    (own_text,) = whole_call(text_rows, [jax.ShapeDtypeStruct((rows, width), BF)], 1024 * 1024, raw_text)
    two_back = ring_shift(own_text, 2)

    near_first = hidden_projection_matrix.T
    (weight_sent,) = whole_call(
        piece_rows,
        [jax.ShapeDtypeStruct((2, PIECE, width), BF)],
        1024 * 1024,
        piece.astype(jnp.int32)[None],
        near_first,
        return_projection_matrix,
        jnp.pad(hidden_shift_vector, (0, width - hidden))[None, :],
        scalars=1,
        vmem=16,
    )
    both = lax.all_to_all(weight_sent, "zh", 0, 0, tiled=True)
    weight_piece = lax.dynamic_index_in_dim(both, 1 - zh, 0, keepdims=False)

    raw_image = after(raw_image_embedding[0], own_text)

    def half_rows(value, half):
        halves = value.reshape((4, 2, rows) + value.shape[1:])
        return lax.dynamic_index_in_dim(halves, half, 1, keepdims=False).reshape((4 * rows,) + value.shape[1:])

    away_bf = unit_rows(half_rows(raw_image, 1 - zh))[0].astype(BF)
    near_bf = unit_rows(half_rows(raw_image, zh))[0].astype(BF)
    slots = matching_caption_slot[0][:, None]
    away_slots, near_slots = half_rows(slots, 1 - zh), half_rows(slots, zh)
    own_raw = rows_of(raw_image, (x * 2 + zh) * rows, rows)

    def joined(first, second):
        shape = (first.shape[0] + second.shape[0], width)
        return whole_call(side_by_side, [jax.ShapeDtypeStruct(shape, BF)], 1024, first, second)[0]

    pair = joined(after(own_text, weight_sent, away_bf, near_bf, away_slots, near_slots, own_raw), two_back)
    pair_on = ring_shift(pair, 1)

    factor_row = standardize_factor[None, :]

    even_texts = joined(pair, pair_on)
    odd_texts = outer_on(even_texts)
    weights = lax.all_gather(after(weight_piece, odd_texts), ("y", "core"), axis=0, tiled=True)
    away_bf, near_bf, away_slots, near_slots, own_raw = lax.optimization_barrier(
        (away_bf, near_bf, away_slots, near_slots, own_raw)
    )

    base = jnp.stack([(x * 2 + zh) * rows, lax.axis_index("core")]).astype(jnp.int32)
    scalars = (sharpness_factor, similarity_shift, base)
    half_shape, pair_shape = (4 * rows, width), (4 * rows, 8 * rows)
    pair_flops = 4 * pair_shape[0] * pair_shape[1] * width
    (away_part,) = pair_call(first_pairs, (half_shape,), pair_flops, *scalars, away_bf, away_slots, even_texts, odd_texts)
    away_sum = lax.all_to_all(away_part, "x", 0, 0, tiled=True)
    near_part, even_part, odd_part = pair_call(
        second_pairs,
        (half_shape, half_shape, half_shape),
        2 * pair_flops,
        *scalars,
        near_bf,
        near_slots,
        even_texts,
        odd_texts,
        after(away_bf, away_part),
        away_slots,
    )
    sent = jnp.sum(after(away_sum, near_part).reshape(4, rows, -1).astype(F32), 0).astype(BF)
    came = z_swap(sent)

    features = after(half_rows(aggregated_picture_vectors[0], zh), sent).astype(F32)
    centred = features - jnp.mean(features, axis=-1, keepdims=True)
    inv_std = lax.rsqrt(jnp.mean(centred * centred, axis=-1, keepdims=True) + EPSILON)
    normalized = centred * inv_std
    layer_in = (normalized * standardize_factor + standardize_shift).astype(BF)
    near_slope = gelu_slope(
        jnp.dot(layer_in, hidden_projection_matrix, preferred_element_type=F32) + hidden_shift_vector
    )
    near_sum = lax.all_to_all(after(near_part, layer_in), "x", 0, 0, tiled=True)

    met = even_part.astype(F32) + outer_back(odd_part).astype(F32)
    pair_met = met[: 2 * rows] + ring_shift(met[2 * rows :].astype(BF), -1).astype(F32)
    pair_sent = pair_met[rows:].astype(BF)
    came, normalized, near_slope, layer_in = lax.optimization_barrier((came, normalized, near_slope, layer_in))

    upstream, spread = whole_call(
        upstream_rows,
        [jax.ShapeDtypeStruct((rows, width), F32), jax.ShapeDtypeStruct(half_shape, BF)],
        1024 * 1024,
        near_sum,
        came,
        own_raw,
    )
    upstream_bf = lax.all_to_all(spread, "x", 0, 0, tiled=True)

    (ln_part,) = whole_call(
        mlp_back,
        [jax.ShapeDtypeStruct(half_shape, BF)],
        8 * 4 * rows * HALF * width,
        after(upstream_bf, pair_sent),
        factor_row,
        inv_std,
        fetched=(
            return_projection_matrix,
            near_slope,
            layer_in,
            weights,
            near_first,
            normalized,
        ),
        vmem=58,
    )
    parts_x = lax.all_to_all(ln_part, "x", 0, 0, tiled=True)
    d_pooled = upstream + jnp.sum(parts_x.reshape(4, rows, -1).astype(F32), 0)

    text_grad = pair_met[:rows] + ring_shift(pair_sent, -2).astype(F32)
    text_units, text_norms = unit_rows(raw_text.astype(F32))
    d_text = norm_back(text_grad, text_units, text_norms).astype(BF)
    return (d_pooled.astype(BF)[None], d_text[None])


def solution(mesh):
    fine = Mesh(mesh.devices.reshape([size for _, size in AXES]), [name for name, _ in AXES])
    placed = (
        P(OUTER, None, None),
        P(OUTER, None, None),
        P(OUTER, INNER, None),
        P(OUTER, None),
        P(),
        P(),
        P(None, INNER),
        P(INNER),
        P(INNER, None),
        P(),
        P(),
    )
    return jax.shard_map(
        local,
        mesh=fine,
        in_specs=placed,
        out_specs=(P(OUTER, INNER, None), P(OUTER, INNER, None)),
        check_vma=False,
    )
```

```python
import jax
import jax.numpy as jnp
from jax import lax
from jax.experimental import pallas as pl
from jax.experimental.pallas import tpu as pltpu
from jax.sharding import Mesh
from jax.sharding import PartitionSpec as P

SQRT_TWO_PI = 0.7978845608028654
CUBIC = 0.044715
EPSILON = 1e-06

AXES = (("x", 4), ("zh", 2), ("zl", 8), ("y", 8), ("core", 2))
SIZE = dict(AXES)
INNER = ("x", "zh")
OUTER = ("zl", "y", "core")
RING = ("zh", "zl", "y")
TXT = 48
PIECE = 72
HALF = 8 * PIECE
BF = jnp.bfloat16
F32 = jnp.float32


def permute(value, axes, target):
    count = 1
    for axis in axes:
        count *= SIZE[axis]
    return lax.ppermute(value, axes, [(source, target(source) % count) for source in range(count)])


def ring_shift(value, steps):
    return permute(value, RING, lambda at: at + steps)


def z_swap(value):
    return permute(value, ("zh",), lambda at: 1 - at)


def core_swap(value):
    return permute(value, ("core",), lambda at: 1 - at)


def z_mirror(value):
    return permute(value, ("zh", "zl"), lambda at: 15 - at)


def far_forward(value):
    return permute(value, RING + ("core",), lambda at: at + 1 if at % 2 == 0 else at + 7)


def outer_back(value):
    return permute(value, RING + ("core",), lambda at: at - 1)


def dot_nt(a, b):
    return lax.dot_general(a, b, (((1,), (1,)), ((), ())), preferred_element_type=F32)


def dot_tn(a, b):
    return lax.dot_general(a, b, (((0,), (0,)), ((), ())), preferred_element_type=F32)


def gelu_slope(pre_values):
    tangent = jnp.tanh(SQRT_TWO_PI * (pre_values + CUBIC * pre_values**3))
    return 0.5 * (1.0 + tangent) + 0.5 * pre_values * (1.0 - tangent * tangent) * SQRT_TWO_PI * (
        1.0 + 3.0 * CUBIC * pre_values * pre_values
    )


def unit_rows(row_block):
    row_norms = jnp.sqrt(jnp.sum(row_block * row_block, axis=-1, keepdims=True))
    return (row_block / row_norms, row_norms)


def norm_back(grad, units, norms):
    return (grad - units * jnp.sum(units * grad, axis=-1, keepdims=True)) / norms


def rows_of(value, start, count):
    return lax.dynamic_slice_in_dim(value, start, count, 0)


def after(value, *others):
    return lax.optimization_barrier((value,) + others)[0]


def half_images(raw, slots, half, images, spots):
    line = slots[...].astype(F32)
    here = lax.broadcasted_iota(jnp.int32, (TXT, TXT), 0) == lax.broadcasted_iota(jnp.int32, (TXT, TXT), 1)
    for at in range(4):
        block = slice(TXT * at, TXT * (at + 1))
        rows = jnp.where(half == 0, raw[2 * at], raw[2 * at + 1])
        images[block, :] = unit_rows(rows)[0].astype(BF)
        low, high = (line[:, TXT * (2 * at + side) : TXT * (2 * at + side + 1)] for side in (0, 1))
        spread = jnp.broadcast_to(jnp.where(half == 0, low, high), (TXT, TXT))
        spots[block, :] = jnp.sum(jnp.where(here, spread, 0.0), axis=1, keepdims=True).astype(jnp.int32)


def pair_grads(scale, shift, base, images, spots, texts):
    logits = scale[0] * dot_nt(images[...], texts[...]) + shift[0]
    columns = lax.broadcasted_iota(jnp.int32, logits.shape, 1)
    match = (columns < TXT) & (spots[...] == columns + base[0])
    chance = jax.nn.sigmoid(jnp.where(match, -logits, logits))
    return jnp.where(match, -chance, chance).astype(BF)


def side_by_side(blocks, texts):
    for at, block in enumerate(blocks):
        texts[TXT * at : TXT * (at + 1), :] = block[...]


def first_pairs(scale, shift, base, raw, slots, *refs):
    blocks, (part, texts, images, spots) = refs[:8], refs[8:]
    side_by_side(blocks, texts)
    half_images(raw, slots, 1 - base[2], images, spots)
    pair_grad = pair_grads(scale, shift, base, images, spots, texts)
    part[...] = (scale[0] * jnp.dot(pair_grad, texts[...], preferred_element_type=F32)).astype(BF)


def second_pairs(scale, shift, base, raw, slots, *refs):
    blocks, (part, even, odd, texts, images, spots) = refs[:8], refs[9:]
    side_by_side(blocks, texts)
    half_images(raw, slots, base[2], images, spots)
    pair_grad = pair_grads(scale, shift, base, images, spots, texts)
    part[...] = (scale[0] * jnp.dot(pair_grad, texts[...], preferred_element_type=F32)).astype(BF)
    total = dot_tn(pair_grad, images[...])
    half_images(raw, slots, 1 - base[2], images, spots)
    pair_grad = pair_grads(scale, shift, base, images, spots, texts)
    total = scale[0] * (total + dot_tn(pair_grad, images[...]))
    even[...] = total[: 4 * TXT].astype(BF)
    far, swap_two, swap_one, swap_three = (total[TXT * at : TXT * (at + 1)] for at in range(4, 8))
    on_one = base[1] == 1
    odd[:TXT] = jnp.where(on_one, far, swap_one).astype(BF)
    odd[TXT : 2 * TXT] = jnp.where(on_one, swap_two, swap_three).astype(BF)
    odd[2 * TXT : 3 * TXT] = jnp.where(on_one, swap_one, swap_two).astype(BF)
    odd[3 * TXT :] = jnp.where(on_one, swap_three, far).astype(BF)


def upstream_rows(sums, came, raw, upstream, spread):
    grad = came[...].astype(F32)
    for at in range(4):
        grad = grad + sums[TXT * at : TXT * (at + 1), :].astype(F32)
    units, norms = unit_rows(raw[...])
    rows = norm_back(grad, units, norms)
    upstream[...] = rows
    for at in range(4):
        spread[TXT * at : TXT * (at + 1), :] = rows.astype(BF)


def text_rows(raw, out, norms):
    units, norms[...] = unit_rows(raw[...].astype(F32))
    out[...] = units.astype(BF)


def piece_rows(at, first, second, shift, out):
    hidden, start = first.shape[0], at[0] * PIECE
    picks = lax.broadcasted_iota(jnp.int32, (PIECE, hidden), 0) + start
    units_at = lax.broadcasted_iota(jnp.int32, (PIECE, hidden), 1)
    value = jnp.dot(
        jnp.where(picks == units_at, 1.0, 0.0).astype(BF), first[...], preferred_element_type=F32
    ) + jnp.dot(jnp.where(picks - HALF == units_at, 1.0, 0.0).astype(BF), second[...], preferred_element_type=F32)
    rows = lax.broadcasted_iota(jnp.int32, value.shape, 0) + start
    left = shift[...]
    for term_at in range(3):
        term = left.astype(BF).astype(F32)
        left = left - term
        value = value + jnp.where(rows == hidden + term_at, term, 0.0)
    out[...] = value.astype(BF)


def mlp_back(up, factor, inv_std, *refs):
    count = 6
    sources, out, held, done = refs[:count], refs[count], refs[count + 1 : -1], refs[-1]
    near_second, near_slope, layer_in, far_weights, near_first, normalized = held
    copies = [pltpu.make_async_copy(a, b, done.at[at]) for at, (a, b) in enumerate(zip(sources, held))]
    for copy in copies:
        copy.start()
    hidden = near_second.shape[0]
    copies[0].wait()
    near_back = dot_nt(up[...], near_second[...])
    copies[1].wait()
    near_act = (near_back * near_slope[...]).astype(BF)
    copies[2].wait()
    copies[3].wait()
    low, high = hidden // 16 * 16, (hidden + 3 + 15) // 16 * 16
    spare = far_weights[low:high, :].astype(F32)
    row = lax.broadcasted_iota(jnp.int32, spare.shape, 0) + low
    shift = jnp.sum(jnp.where((row >= hidden) & (row < hidden + 3), spare, 0.0), axis=0, keepdims=True)
    far_slope = gelu_slope(dot_nt(layer_in[...], far_weights[:HALF, :]) + shift[:, :HALF])
    far_act = (dot_nt(up[...], far_weights[HALF:, :]) * far_slope).astype(BF)
    copies[4].wait()
    copies[5].wait()
    back = jnp.dot(near_act, near_first[...], preferred_element_type=F32)
    back = (back + jnp.dot(far_act, far_weights[:HALF, :], preferred_element_type=F32)) * factor[...]
    first_mean = jnp.mean(back, axis=-1, keepdims=True)
    second_mean = jnp.mean(back * normalized[...], axis=-1, keepdims=True)
    out[...] = ((back - first_mean - normalized[...] * second_mean) * inv_std[...]).astype(BF)


def whole_call(kernel, outs, flops, *operands, fetched=(), scalars=0, vmem=8):
    whole = pl.BlockSpec(memory_space=pltpu.VMEM)
    specs = [pl.BlockSpec(memory_space=pltpu.SMEM)] * scalars + [whole] * (len(operands) - scalars)
    scratch = [pltpu.VMEM(value.shape, value.dtype) for value in fetched]
    if fetched:
        scratch.append(pltpu.SemaphoreType.DMA((len(fetched),)))
    return pl.pallas_call(
        kernel,
        out_shape=outs,
        in_specs=specs + [pl.BlockSpec(memory_space=pl.ANY)] * len(fetched),
        out_specs=[whole] * len(outs),
        scratch_shapes=scratch,
        compiler_params=pltpu.CompilerParams(vmem_limit_bytes=vmem * 1024 * 1024),
        cost_estimate=pl.CostEstimate(flops=flops, bytes_accessed=1024 * 1024, transcendentals=0),
    )(*operands, *fetched)


def pair_call(kernel, outs, flops, vmem, *operands):
    scalar = pl.BlockSpec(memory_space=pltpu.SMEM)
    whole = pl.BlockSpec(memory_space=pltpu.VMEM)
    width = operands[3].shape[2]
    return pl.pallas_call(
        kernel,
        out_shape=[jax.ShapeDtypeStruct(shape, BF) for shape in outs],
        in_specs=[scalar] * 3 + [whole] * (len(operands) - 3),
        out_specs=[whole] * len(outs),
        scratch_shapes=[
            pltpu.VMEM((8 * TXT, width), BF),
            pltpu.VMEM((4 * TXT, width), BF),
            pltpu.VMEM((4 * TXT, 1), jnp.int32),
        ],
        compiler_params=pltpu.CompilerParams(vmem_limit_bytes=vmem * 1024 * 1024),
        cost_estimate=pl.CostEstimate(flops=flops, bytes_accessed=3 * 1024 * 1024, transcendentals=192 * 384),
    )(*operands)


def local(
    aggregated_picture_vectors,
    raw_image_embedding,
    raw_caption_embedding,
    matching_caption_slot,
    standardize_factor,
    standardize_shift,
    hidden_projection_matrix,
    hidden_shift_vector,
    return_projection_matrix,
    sharpness_factor,
    similarity_shift,
):
    x = lax.axis_index("x")
    zh = lax.axis_index("zh")
    piece = lax.axis_index("y") * 2 + lax.axis_index("core")
    hidden = hidden_shift_vector.shape[0]

    raw_text = raw_caption_embedding[0]
    rows, width = raw_text.shape
    own_text, text_norms = whole_call(
        text_rows,
        [jax.ShapeDtypeStruct((rows, width), BF), jax.ShapeDtypeStruct((rows, 1), F32)],
        1024 * 1024,
        raw_text,
    )
    three = ring_shift(own_text, 3)

    near_first = hidden_projection_matrix.T
    (weight_sent,) = whole_call(
        piece_rows,
        [jax.ShapeDtypeStruct((PIECE, width), BF)],
        1024 * 1024,
        piece.astype(jnp.int32)[None],
        near_first,
        return_projection_matrix,
        jnp.pad(hidden_shift_vector, (0, width - hidden))[None, :],
        scalars=1,
        vmem=54,
    )
    weight_piece = z_mirror(weight_sent)
    own_later = after(own_text, weight_sent)
    far = far_forward(own_later)
    two = ring_shift(own_later, 2)
    one = ring_shift(own_later, 1)

    raw_image = raw_image_embedding[0]
    raw_blocks = raw_image.reshape(8, rows, width)
    swaps = (core_swap(two), core_swap(one), core_swap(after(three, far)))
    blocks = (own_text, two, one, three, far) + swaps
    weights = lax.all_gather(after(weight_piece, far, *swaps), ("y", "core"), axis=0, tiled=True)
    factor_row = standardize_factor[None, :]

    def half_rows(value, half):
        halves = value.reshape((4, 2, rows) + value.shape[1:])
        return lax.dynamic_index_in_dim(halves, half, 1, keepdims=False).reshape((4 * rows,) + value.shape[1:])

    base = jnp.stack([(x * 2 + zh) * rows, lax.axis_index("core"), zh]).astype(jnp.int32)
    scalars = (sharpness_factor, similarity_shift, base)
    half_shape = (4 * rows, width)
    pair_flops = 4 * half_shape[0] * 8 * rows * width
    (away_part,) = pair_call(first_pairs, (half_shape,), pair_flops, 20, *scalars, raw_blocks, matching_caption_slot, *blocks)
    away_sum = lax.all_to_all(away_part, "x", 0, 0, tiled=True)
    near_part, even_part, odd_part = pair_call(
        second_pairs,
        (half_shape, half_shape, half_shape),
        2 * pair_flops,
        54,
        *scalars,
        raw_blocks,
        matching_caption_slot,
        *blocks,
        away_part,
    )
    sent = jnp.sum(after(away_sum, near_part).reshape(4, rows, -1).astype(F32), 0).astype(BF)
    came = z_swap(sent)

    features = after(half_rows(aggregated_picture_vectors[0], zh), sent).astype(F32)
    centred = features - jnp.mean(features, axis=-1, keepdims=True)
    inv_std = lax.rsqrt(jnp.mean(centred * centred, axis=-1, keepdims=True) + EPSILON)
    normalized = centred * inv_std
    layer_in = (normalized * standardize_factor + standardize_shift).astype(BF)
    near_slope = gelu_slope(
        jnp.dot(layer_in, hidden_projection_matrix, preferred_element_type=F32) + hidden_shift_vector
    )
    own_raw = rows_of(raw_image, (x * 2 + zh) * rows, rows)
    near_sum = lax.all_to_all(after(near_part, layer_in, own_raw), "x", 0, 0, tiled=True)

    met = even_part.astype(F32) + outer_back(odd_part).astype(F32)
    pair_met = met[: 2 * rows] + ring_shift(met[2 * rows :].astype(BF), -1).astype(F32)
    pair_sent = pair_met[rows:].astype(BF)
    came, normalized, near_slope, layer_in = lax.optimization_barrier((came, normalized, near_slope, layer_in))

    upstream, spread = whole_call(
        upstream_rows,
        [jax.ShapeDtypeStruct((rows, width), F32), jax.ShapeDtypeStruct(half_shape, BF)],
        1024 * 1024,
        near_sum,
        came,
        own_raw,
    )
    upstream_bf = lax.all_to_all(spread, "x", 0, 0, tiled=True)

    (ln_part,) = whole_call(
        mlp_back,
        [jax.ShapeDtypeStruct(half_shape, BF)],
        8 * 4 * rows * HALF * width,
        upstream_bf,
        factor_row,
        inv_std,
        fetched=(
            return_projection_matrix,
            near_slope,
            layer_in,
            weights,
            near_first,
            normalized,
        ),
        vmem=58,
    )
    parts_x = lax.all_to_all(ln_part, "x", 0, 0, tiled=True)
    d_pooled = upstream + jnp.sum(parts_x.reshape(4, rows, -1).astype(F32), 0)

    text_grad = pair_met[:rows] + ring_shift(after(pair_sent, ln_part), -2).astype(F32)
    text_units = raw_text.astype(F32) / text_norms
    d_text = norm_back(text_grad, text_units, text_norms).astype(BF)
    return (d_pooled.astype(BF)[None], d_text[None])


def solution(mesh):
    fine = Mesh(mesh.devices.reshape([size for _, size in AXES]), [name for name, _ in AXES])
    placed = (
        P(OUTER, None, None),
        P(OUTER, None, None),
        P(OUTER, INNER, None),
        P(OUTER, None),
        P(),
        P(),
        P(None, INNER),
        P(INNER),
        P(INNER, None),
        P(),
        P(),
    )
    return jax.shard_map(
        local,
        mesh=fine,
        in_specs=placed,
        out_specs=(P(OUTER, INNER, None), P(OUTER, INNER, None)),
        check_vma=False,
    )
```

```python
import jax
import jax.numpy as jnp
from jax import lax
from jax.experimental import pallas as pl
from jax.experimental.pallas import tpu as pltpu
from jax.sharding import Mesh
from jax.sharding import PartitionSpec as P

SQRT_TWO_PI = 0.7978845608028654
CUBIC = 0.044715
EPSILON = 1e-06

AXES = (("x", 4), ("zh", 2), ("zl", 8), ("y", 8), ("core", 2))
SIZE = dict(AXES)
INNER = ("x", "zh")
OUTER = ("zl", "y", "core")
RING = ("zh", "zl", "y")
TXT = 48
PIECE = 72
HALF = 8 * PIECE
BF = jnp.bfloat16
F32 = jnp.float32


def permute(value, axes, target):
    count = 1
    for axis in axes:
        count *= SIZE[axis]
    return lax.ppermute(value, axes, [(source, target(source) % count) for source in range(count)])


def ring_shift(value, steps):
    return permute(value, RING, lambda at: at + steps)


def z_swap(value):
    return permute(value, ("zh",), lambda at: 1 - at)


def core_swap(value):
    return permute(value, ("core",), lambda at: 1 - at)


def z_mirror(value):
    return permute(value, ("zh", "zl"), lambda at: 15 - at)


def far_forward(value):
    return permute(value, RING + ("core",), lambda at: at + 1 if at % 2 == 0 else at + 7)


def outer_back(value):
    return permute(value, RING + ("core",), lambda at: at - 1)


def dot_nt(a, b):
    return lax.dot_general(a, b, (((1,), (1,)), ((), ())), preferred_element_type=F32)


def dot_tn(a, b):
    return lax.dot_general(a, b, (((0,), (0,)), ((), ())), preferred_element_type=F32)


def gelu_slope(pre_values):
    tangent = jnp.tanh(SQRT_TWO_PI * (pre_values + CUBIC * pre_values**3))
    return 0.5 * (1.0 + tangent) + 0.5 * pre_values * (1.0 - tangent * tangent) * SQRT_TWO_PI * (
        1.0 + 3.0 * CUBIC * pre_values * pre_values
    )


def unit_rows(row_block):
    row_norms = jnp.sqrt(jnp.sum(row_block * row_block, axis=-1, keepdims=True))
    return (row_block / row_norms, row_norms)


def norm_back(grad, units, norms):
    return (grad - units * jnp.sum(units * grad, axis=-1, keepdims=True)) / norms


def rows_of(value, start, count):
    return lax.dynamic_slice_in_dim(value, start, count, 0)


def after(value, *others):
    return lax.optimization_barrier((value,) + others)[0]


def half_images(raw, slots, half, images, spots):
    line = slots[...].astype(F32)
    here = lax.broadcasted_iota(jnp.int32, (TXT, TXT), 0) == lax.broadcasted_iota(jnp.int32, (TXT, TXT), 1)
    for at in range(4):
        block = slice(TXT * at, TXT * (at + 1))
        rows = jnp.where(half == 0, raw[2 * at], raw[2 * at + 1])
        images[block, :] = unit_rows(rows)[0].astype(BF)
        low, high = (line[:, TXT * (2 * at + side) : TXT * (2 * at + side + 1)] for side in (0, 1))
        spread = jnp.broadcast_to(jnp.where(half == 0, low, high), (TXT, TXT))
        spots[block, :] = jnp.sum(jnp.where(here, spread, 0.0), axis=1, keepdims=True).astype(jnp.int32)


def pair_grads(scale, shift, base, images, spots, texts):
    logits = scale[0] * dot_nt(images[...], texts[...]) + shift[0]
    columns = lax.broadcasted_iota(jnp.int32, logits.shape, 1)
    match = (columns < TXT) & (spots[...] == columns + base[0])
    chance = jax.nn.sigmoid(jnp.where(match, -logits, logits))
    return jnp.where(match, -chance, chance).astype(BF)


def side_by_side(blocks, texts):
    for at, block in enumerate(blocks):
        texts[TXT * at : TXT * (at + 1), :] = block[...]


def first_pairs(scale, shift, base, raw, slots, *refs):
    blocks, (part, texts, images, spots) = refs[:8], refs[8:]
    side_by_side(blocks, texts)
    half_images(raw, slots, 1 - base[2], images, spots)
    pair_grad = pair_grads(scale, shift, base, images, spots, texts)
    part[...] = (scale[0] * jnp.dot(pair_grad, texts[...], preferred_element_type=F32)).astype(BF)


def second_pairs(scale, shift, base, raw, slots, *refs):
    blocks, (part, even, odd, texts, images, spots) = refs[:8], refs[9:]
    side_by_side(blocks, texts)
    half_images(raw, slots, base[2], images, spots)
    pair_grad = pair_grads(scale, shift, base, images, spots, texts)
    part[...] = (scale[0] * jnp.dot(pair_grad, texts[...], preferred_element_type=F32)).astype(BF)
    total = dot_tn(pair_grad, images[...])
    half_images(raw, slots, 1 - base[2], images, spots)
    pair_grad = pair_grads(scale, shift, base, images, spots, texts)
    total = scale[0] * (total + dot_tn(pair_grad, images[...]))
    even[...] = total[: 4 * TXT].astype(BF)
    far, swap_two, swap_one, swap_three = (total[TXT * at : TXT * (at + 1)] for at in range(4, 8))
    on_one = base[1] == 1
    odd[:TXT] = jnp.where(on_one, far, swap_one).astype(BF)
    odd[TXT : 2 * TXT] = jnp.where(on_one, swap_two, swap_three).astype(BF)
    odd[2 * TXT : 3 * TXT] = jnp.where(on_one, swap_one, swap_two).astype(BF)
    odd[3 * TXT :] = jnp.where(on_one, swap_three, far).astype(BF)


def upstream_rows(sums, came, raw, upstream, spread):
    grad = came[...].astype(F32)
    for at in range(4):
        grad = grad + sums[TXT * at : TXT * (at + 1), :].astype(F32)
    units, norms = unit_rows(raw[...])
    rows = norm_back(grad, units, norms)
    upstream[...] = rows
    for at in range(4):
        spread[TXT * at : TXT * (at + 1), :] = rows.astype(BF)


def text_rows(raw, out):
    out[...] = unit_rows(raw[...].astype(F32))[0].astype(BF)


def piece_rows(at, first, second, shift, out):
    hidden, start = first.shape[0], at[0] * PIECE
    picks = lax.broadcasted_iota(jnp.int32, (PIECE, hidden), 0) + start
    units_at = lax.broadcasted_iota(jnp.int32, (PIECE, hidden), 1)
    value = jnp.dot(
        jnp.where(picks == units_at, 1.0, 0.0).astype(BF), first[...], preferred_element_type=F32
    ) + jnp.dot(jnp.where(picks - HALF == units_at, 1.0, 0.0).astype(BF), second[...], preferred_element_type=F32)
    rows = lax.broadcasted_iota(jnp.int32, value.shape, 0) + start
    left = shift[...]
    for term_at in range(3):
        term = left.astype(BF).astype(F32)
        left = left - term
        value = value + jnp.where(rows == hidden + term_at, term, 0.0)
    out[...] = value.astype(BF)


def mlp_back(up, factor, inv_std, *refs):
    count = 6
    sources, out, held, done = refs[:count], refs[count], refs[count + 1 : -1], refs[-1]
    near_second, near_slope, layer_in, far_weights, near_first, normalized = held
    copies = [pltpu.make_async_copy(a, b, done.at[at]) for at, (a, b) in enumerate(zip(sources, held))]
    for copy in copies:
        copy.start()
    hidden = near_second.shape[0]
    copies[0].wait()
    near_back = dot_nt(up[...], near_second[...])
    copies[1].wait()
    near_act = (near_back * near_slope[...]).astype(BF)
    copies[2].wait()
    copies[3].wait()
    low, high = hidden // 16 * 16, (hidden + 3 + 15) // 16 * 16
    spare = far_weights[low:high, :].astype(F32)
    row = lax.broadcasted_iota(jnp.int32, spare.shape, 0) + low
    shift = jnp.sum(jnp.where((row >= hidden) & (row < hidden + 3), spare, 0.0), axis=0, keepdims=True)
    far_slope = gelu_slope(dot_nt(layer_in[...], far_weights[:HALF, :]) + shift[:, :HALF])
    far_act = (dot_nt(up[...], far_weights[HALF:, :]) * far_slope).astype(BF)
    copies[4].wait()
    copies[5].wait()
    back = jnp.dot(near_act, near_first[...], preferred_element_type=F32)
    back = (back + jnp.dot(far_act, far_weights[:HALF, :], preferred_element_type=F32)) * factor[...]
    first_mean = jnp.mean(back, axis=-1, keepdims=True)
    second_mean = jnp.mean(back * normalized[...], axis=-1, keepdims=True)
    out[...] = ((back - first_mean - normalized[...] * second_mean) * inv_std[...]).astype(BF)


def whole_call(kernel, outs, flops, *operands, fetched=(), scalars=0, vmem=8):
    whole = pl.BlockSpec(memory_space=pltpu.VMEM)
    specs = [pl.BlockSpec(memory_space=pltpu.SMEM)] * scalars + [whole] * (len(operands) - scalars)
    scratch = [pltpu.VMEM(value.shape, value.dtype) for value in fetched]
    if fetched:
        scratch.append(pltpu.SemaphoreType.DMA((len(fetched),)))
    return pl.pallas_call(
        kernel,
        out_shape=outs,
        in_specs=specs + [pl.BlockSpec(memory_space=pl.ANY)] * len(fetched),
        out_specs=[whole] * len(outs),
        scratch_shapes=scratch,
        compiler_params=pltpu.CompilerParams(vmem_limit_bytes=vmem * 1024 * 1024),
        cost_estimate=pl.CostEstimate(flops=flops, bytes_accessed=1024 * 1024, transcendentals=0),
    )(*operands, *fetched)


def pair_call(kernel, outs, flops, vmem, *operands):
    scalar = pl.BlockSpec(memory_space=pltpu.SMEM)
    whole = pl.BlockSpec(memory_space=pltpu.VMEM)
    width = operands[3].shape[2]
    return pl.pallas_call(
        kernel,
        out_shape=[jax.ShapeDtypeStruct(shape, BF) for shape in outs],
        in_specs=[scalar] * 3 + [whole] * (len(operands) - 3),
        out_specs=[whole] * len(outs),
        scratch_shapes=[
            pltpu.VMEM((8 * TXT, width), BF),
            pltpu.VMEM((4 * TXT, width), BF),
            pltpu.VMEM((4 * TXT, 1), jnp.int32),
        ],
        compiler_params=pltpu.CompilerParams(vmem_limit_bytes=vmem * 1024 * 1024),
        cost_estimate=pl.CostEstimate(flops=flops, bytes_accessed=3 * 1024 * 1024, transcendentals=192 * 384),
    )(*operands)


def local(
    aggregated_picture_vectors,
    raw_image_embedding,
    raw_caption_embedding,
    matching_caption_slot,
    standardize_factor,
    standardize_shift,
    hidden_projection_matrix,
    hidden_shift_vector,
    return_projection_matrix,
    sharpness_factor,
    similarity_shift,
):
    x = lax.axis_index("x")
    zh = lax.axis_index("zh")
    piece = lax.axis_index("y") * 2 + lax.axis_index("core")
    hidden = hidden_shift_vector.shape[0]

    raw_text = raw_caption_embedding[0]
    rows, width = raw_text.shape
    (own_text,) = whole_call(text_rows, [jax.ShapeDtypeStruct((rows, width), BF)], 1024 * 1024, raw_text)
    one = ring_shift(own_text, 1)
    far = far_forward(own_text)
    three = ring_shift(own_text, 3)
    two = ring_shift(own_text, 2)

    near_first = hidden_projection_matrix.T
    (weight_sent,) = whole_call(
        piece_rows,
        [jax.ShapeDtypeStruct((PIECE, width), BF)],
        1024 * 1024,
        after(piece.astype(jnp.int32)[None], one),
        near_first,
        return_projection_matrix,
        jnp.pad(after(hidden_shift_vector, one), (0, width - hidden))[None, :],
        scalars=1,
        vmem=54,
    )
    weight_piece = z_mirror(weight_sent)
    raw_image = raw_image_embedding[0]
    raw_blocks = raw_image.reshape(8, rows, width)
    swaps = (core_swap(two), core_swap(one), core_swap(after(three, far)))
    blocks = (own_text, two, one, three, far) + swaps
    factor_row = standardize_factor[None, :]

    def half_rows(value, half):
        halves = value.reshape((4, 2, rows) + value.shape[1:])
        return lax.dynamic_index_in_dim(halves, half, 1, keepdims=False).reshape((4 * rows,) + value.shape[1:])

    base = jnp.stack([(x * 2 + zh) * rows, lax.axis_index("core"), zh]).astype(jnp.int32)
    scalars = (sharpness_factor, similarity_shift, base)
    half_shape = (4 * rows, width)
    pair_flops = 4 * half_shape[0] * 8 * rows * width
    (away_part,) = pair_call(first_pairs, (half_shape,), pair_flops, 20, *scalars, raw_blocks, matching_caption_slot, *blocks)
    away_sum = lax.all_to_all(away_part, "x", 0, 0, tiled=True)
    near_part, even_part, odd_part = pair_call(
        second_pairs,
        (half_shape, half_shape, half_shape),
        2 * pair_flops,
        54,
        *scalars,
        raw_blocks,
        matching_caption_slot,
        *blocks,
        away_part,
    )
    weights = lax.all_gather(after(weight_piece, away_part), ("y", "core"), axis=0, tiled=True)
    sent = jnp.sum(after(away_sum, near_part).reshape(4, rows, -1).astype(F32), 0).astype(BF)
    came = z_swap(sent)

    features = after(half_rows(aggregated_picture_vectors[0], zh), sent).astype(F32)
    centred = features - jnp.mean(features, axis=-1, keepdims=True)
    inv_std = lax.rsqrt(jnp.mean(centred * centred, axis=-1, keepdims=True) + EPSILON)
    normalized = centred * inv_std
    layer_in = (normalized * standardize_factor + standardize_shift).astype(BF)
    near_slope = gelu_slope(
        jnp.dot(layer_in, hidden_projection_matrix, preferred_element_type=F32) + hidden_shift_vector
    )
    own_raw = rows_of(raw_image, (x * 2 + zh) * rows, rows)
    near_sum = lax.all_to_all(after(near_part, layer_in, own_raw), "x", 0, 0, tiled=True)

    met = even_part.astype(F32) + outer_back(odd_part).astype(F32)
    pair_met = met[: 2 * rows] + ring_shift(met[2 * rows :].astype(BF), -1).astype(F32)
    pair_sent = pair_met[rows:].astype(BF)
    _, text_norms = unit_rows(after(raw_text, sent).astype(F32))
    came, normalized, near_slope, layer_in, text_norms = lax.optimization_barrier(
        (came, normalized, near_slope, layer_in, text_norms)
    )

    upstream, spread = whole_call(
        upstream_rows,
        [jax.ShapeDtypeStruct((rows, width), F32), jax.ShapeDtypeStruct(half_shape, BF)],
        1024 * 1024,
        near_sum,
        came,
        own_raw,
    )
    upstream_bf = lax.all_to_all(spread, "x", 0, 0, tiled=True)

    (ln_part,) = whole_call(
        mlp_back,
        [jax.ShapeDtypeStruct(half_shape, BF)],
        8 * 4 * rows * HALF * width,
        upstream_bf,
        factor_row,
        inv_std,
        fetched=(
            return_projection_matrix,
            near_slope,
            layer_in,
            weights,
            near_first,
            normalized,
        ),
        vmem=58,
    )
    parts_x = lax.all_to_all(ln_part, "x", 0, 0, tiled=True)
    d_pooled = upstream + jnp.sum(parts_x.reshape(4, rows, -1).astype(F32), 0)

    text_grad = pair_met[:rows] + ring_shift(after(pair_sent, ln_part), -2).astype(F32)
    text_units = raw_text.astype(F32) / text_norms
    d_text = norm_back(text_grad, text_units, text_norms).astype(BF)
    return (d_pooled.astype(BF)[None], d_text[None])


def solution(mesh):
    fine = Mesh(mesh.devices.reshape([size for _, size in AXES]), [name for name, _ in AXES])
    placed = (
        P(OUTER, None, None),
        P(OUTER, None, None),
        P(OUTER, INNER, None),
        P(OUTER, None),
        P(),
        P(),
        P(None, INNER),
        P(INNER),
        P(INNER, None),
        P(),
        P(),
    )
    return jax.shard_map(
        local,
        mesh=fine,
        in_specs=placed,
        out_specs=(P(OUTER, INNER, None), P(OUTER, INNER, None)),
        check_vma=False,
    )
```

```python
import jax
import jax.numpy as jnp
from jax import lax
from jax.experimental import pallas as pl
from jax.experimental.pallas import tpu as pltpu
from jax.sharding import Mesh
from jax.sharding import PartitionSpec as P

SQRT_TWO_PI = 0.7978845608028654
CUBIC = 0.044715
EPSILON = 1e-06

AXES = (("x", 4), ("zh", 2), ("zl", 8), ("y", 8), ("core", 2))
SIZE = dict(AXES)
INNER = ("x", "zh")
OUTER = ("zl", "y", "core")
RING = ("zh", "zl", "y")
TXT = 48
PIECE = 72
HALF = 8 * PIECE
BF = jnp.bfloat16
F32 = jnp.float32


def permute(value, axes, target):
    count = 1
    for axis in axes:
        count *= SIZE[axis]
    return lax.ppermute(value, axes, [(source, target(source) % count) for source in range(count)])


def ring_shift(value, steps):
    return permute(value, RING, lambda at: at + steps)


def z_swap(value):
    return permute(value, ("zh",), lambda at: 1 - at)


def core_swap(value):
    return permute(value, ("core",), lambda at: 1 - at)


def z_mirror(value):
    return permute(value, ("zh", "zl"), lambda at: 15 - at)


def far_forward(value):
    return permute(value, RING + ("core",), lambda at: at + 1 if at % 2 == 0 else at + 7)


def outer_back(value):
    return permute(value, RING + ("core",), lambda at: at - 1)


def dot_nt(a, b):
    return lax.dot_general(a, b, (((1,), (1,)), ((), ())), preferred_element_type=F32)


def dot_tn(a, b):
    return lax.dot_general(a, b, (((0,), (0,)), ((), ())), preferred_element_type=F32)


def gelu_slope(pre_values):
    tangent = jnp.tanh(SQRT_TWO_PI * (pre_values + CUBIC * pre_values**3))
    return 0.5 * (1.0 + tangent) + 0.5 * pre_values * (1.0 - tangent * tangent) * SQRT_TWO_PI * (
        1.0 + 3.0 * CUBIC * pre_values * pre_values
    )


def unit_rows(row_block):
    row_norms = jnp.sqrt(jnp.sum(row_block * row_block, axis=-1, keepdims=True))
    return (row_block / row_norms, row_norms)


def norm_back(grad, units, norms):
    return (grad - units * jnp.sum(units * grad, axis=-1, keepdims=True)) / norms


def rows_of(value, start, count):
    return lax.dynamic_slice_in_dim(value, start, count, 0)


def after(value, *others):
    return lax.optimization_barrier((value,) + others)[0]


def half_images(raw, slots, half, images, spots):
    line = slots[...].astype(F32)
    here = lax.broadcasted_iota(jnp.int32, (TXT, TXT), 0) == lax.broadcasted_iota(jnp.int32, (TXT, TXT), 1)
    for at in range(4):
        block = slice(TXT * at, TXT * (at + 1))
        rows = jnp.where(half == 0, raw[2 * at], raw[2 * at + 1])
        images[block, :] = unit_rows(rows)[0].astype(BF)
        low, high = (line[:, TXT * (2 * at + side) : TXT * (2 * at + side + 1)] for side in (0, 1))
        spread = jnp.broadcast_to(jnp.where(half == 0, low, high), (TXT, TXT))
        spots[block, :] = jnp.sum(jnp.where(here, spread, 0.0), axis=1, keepdims=True).astype(jnp.int32)


def pair_grads(scale, shift, base, images, spots, texts):
    logits = scale[0] * dot_nt(images[...], texts[...]) + shift[0]
    columns = lax.broadcasted_iota(jnp.int32, logits.shape, 1)
    match = (columns < TXT) & (spots[...] == columns + base[0])
    chance = jax.nn.sigmoid(jnp.where(match, -logits, logits))
    return jnp.where(match, -chance, chance).astype(BF)


def side_by_side(blocks, texts):
    for at, block in enumerate(blocks):
        texts[TXT * at : TXT * (at + 1), :] = block[...]


def first_pairs(scale, shift, base, raw, slots, *refs):
    blocks, (part, texts, images, spots) = refs[:8], refs[8:]
    side_by_side(blocks, texts)
    half_images(raw, slots, 1 - base[2], images, spots)
    pair_grad = pair_grads(scale, shift, base, images, spots, texts)
    part[...] = (scale[0] * jnp.dot(pair_grad, texts[...], preferred_element_type=F32)).astype(BF)


def second_pairs(scale, shift, base, raw, slots, *refs):
    blocks, (part, even, odd, texts, images, spots) = refs[:8], refs[9:]
    side_by_side(blocks, texts)
    half_images(raw, slots, base[2], images, spots)
    pair_grad = pair_grads(scale, shift, base, images, spots, texts)
    part[...] = (scale[0] * jnp.dot(pair_grad, texts[...], preferred_element_type=F32)).astype(BF)
    total = dot_tn(pair_grad, images[...])
    half_images(raw, slots, 1 - base[2], images, spots)
    pair_grad = pair_grads(scale, shift, base, images, spots, texts)
    total = scale[0] * (total + dot_tn(pair_grad, images[...]))
    even[...] = total[: 4 * TXT].astype(BF)
    far, swap_two, swap_one, swap_three = (total[TXT * at : TXT * (at + 1)] for at in range(4, 8))
    on_one = base[1] == 1
    odd[:TXT] = jnp.where(on_one, far, swap_one).astype(BF)
    odd[TXT : 2 * TXT] = jnp.where(on_one, swap_two, swap_three).astype(BF)
    odd[2 * TXT : 3 * TXT] = jnp.where(on_one, swap_one, swap_two).astype(BF)
    odd[3 * TXT :] = jnp.where(on_one, swap_three, far).astype(BF)


def upstream_rows(sums, came, raw, upstream, spread):
    grad = came[...].astype(F32)
    for at in range(4):
        grad = grad + sums[TXT * at : TXT * (at + 1), :].astype(F32)
    units, norms = unit_rows(raw[...])
    rows = norm_back(grad, units, norms)
    upstream[...] = rows
    for at in range(4):
        spread[TXT * at : TXT * (at + 1), :] = rows.astype(BF)


def slope_rows(layer_in, near_first, hidden_shift, near_slope):
    near_slope[...] = gelu_slope(dot_nt(layer_in[...], near_first[...]) + hidden_shift[...])


def text_back(grad, last, raw, out):
    units, norms = unit_rows(raw[...].astype(F32))
    out[...] = norm_back(grad[...] + last[...].astype(F32), units, norms).astype(BF)


def text_rows(raw, out):
    out[...] = unit_rows(raw[...].astype(F32))[0].astype(BF)


def piece_rows(at, first, second, shift, out):
    hidden, start = first.shape[0], at[0] * PIECE
    picks = lax.broadcasted_iota(jnp.int32, (PIECE, hidden), 0) + start
    units_at = lax.broadcasted_iota(jnp.int32, (PIECE, hidden), 1)
    value = jnp.dot(
        jnp.where(picks == units_at, 1.0, 0.0).astype(BF), first[...], preferred_element_type=F32
    ) + jnp.dot(jnp.where(picks - HALF == units_at, 1.0, 0.0).astype(BF), second[...], preferred_element_type=F32)
    rows = lax.broadcasted_iota(jnp.int32, value.shape, 0) + start
    left = shift[...]
    for term_at in range(3):
        term = left.astype(BF).astype(F32)
        left = left - term
        value = value + jnp.where(rows == hidden + term_at, term, 0.0)
    out[...] = value.astype(BF)


def mlp_back(up, factor, inv_std, *refs):
    count = 6
    sources, out, held, done = refs[:count], refs[count], refs[count + 1 : -1], refs[-1]
    near_second, near_slope, layer_in, far_weights, near_first, normalized = held
    copies = [pltpu.make_async_copy(a, b, done.at[at]) for at, (a, b) in enumerate(zip(sources, held))]
    for copy in copies:
        copy.start()
    hidden = near_second.shape[0]
    copies[0].wait()
    near_back = dot_nt(up[...], near_second[...])
    copies[1].wait()
    near_act = (near_back * near_slope[...]).astype(BF)
    copies[2].wait()
    copies[3].wait()
    low, high = hidden // 16 * 16, (hidden + 3 + 15) // 16 * 16
    spare = far_weights[low:high, :].astype(F32)
    row = lax.broadcasted_iota(jnp.int32, spare.shape, 0) + low
    shift = jnp.sum(jnp.where((row >= hidden) & (row < hidden + 3), spare, 0.0), axis=0, keepdims=True)
    far_slope = gelu_slope(dot_nt(layer_in[...], far_weights[:HALF, :]) + shift[:, :HALF])
    far_act = (dot_nt(up[...], far_weights[HALF:, :]) * far_slope).astype(BF)
    copies[4].wait()
    copies[5].wait()
    back = jnp.dot(near_act, near_first[...], preferred_element_type=F32)
    back = (back + jnp.dot(far_act, far_weights[:HALF, :], preferred_element_type=F32)) * factor[...]
    first_mean = jnp.mean(back, axis=-1, keepdims=True)
    second_mean = jnp.mean(back * normalized[...], axis=-1, keepdims=True)
    out[...] = ((back - first_mean - normalized[...] * second_mean) * inv_std[...]).astype(BF)


def whole_call(kernel, outs, flops, *operands, fetched=(), scalars=0, vmem=8):
    whole = pl.BlockSpec(memory_space=pltpu.VMEM)
    specs = [pl.BlockSpec(memory_space=pltpu.SMEM)] * scalars + [whole] * (len(operands) - scalars)
    scratch = [pltpu.VMEM(value.shape, value.dtype) for value in fetched]
    if fetched:
        scratch.append(pltpu.SemaphoreType.DMA((len(fetched),)))
    return pl.pallas_call(
        kernel,
        out_shape=outs,
        in_specs=specs + [pl.BlockSpec(memory_space=pl.ANY)] * len(fetched),
        out_specs=[whole] * len(outs),
        scratch_shapes=scratch,
        compiler_params=pltpu.CompilerParams(vmem_limit_bytes=vmem * 1024 * 1024),
        cost_estimate=pl.CostEstimate(flops=flops, bytes_accessed=min(flops, 1024 * 1024), transcendentals=0),
    )(*operands, *fetched)


def pair_call(kernel, outs, flops, vmem, *operands):
    scalar = pl.BlockSpec(memory_space=pltpu.SMEM)
    whole = pl.BlockSpec(memory_space=pltpu.VMEM)
    width = operands[3].shape[2]
    return pl.pallas_call(
        kernel,
        out_shape=[jax.ShapeDtypeStruct(shape, BF) for shape in outs],
        in_specs=[scalar] * 3 + [whole] * (len(operands) - 3),
        out_specs=[whole] * len(outs),
        scratch_shapes=[
            pltpu.VMEM((8 * TXT, width), BF),
            pltpu.VMEM((4 * TXT, width), BF),
            pltpu.VMEM((4 * TXT, 1), jnp.int32),
        ],
        compiler_params=pltpu.CompilerParams(vmem_limit_bytes=vmem * 1024 * 1024),
        cost_estimate=pl.CostEstimate(flops=flops, bytes_accessed=3 * 1024 * 1024, transcendentals=192 * 384),
    )(*operands)


def local(
    aggregated_picture_vectors,
    raw_image_embedding,
    raw_caption_embedding,
    matching_caption_slot,
    standardize_factor,
    standardize_shift,
    hidden_projection_matrix,
    hidden_shift_vector,
    return_projection_matrix,
    sharpness_factor,
    similarity_shift,
):
    x = lax.axis_index("x")
    zh = lax.axis_index("zh")
    piece = lax.axis_index("y") * 2 + lax.axis_index("core")
    hidden = hidden_shift_vector.shape[0]

    raw_text = raw_caption_embedding[0]
    rows, width = raw_text.shape
    (own_text,) = whole_call(text_rows, [jax.ShapeDtypeStruct((rows, width), BF)], 1024 * 1024, raw_text)
    one = ring_shift(own_text, 1)
    far = far_forward(own_text)
    three = ring_shift(own_text, 3)
    two = ring_shift(own_text, 2)

    near_first = hidden_projection_matrix.T
    (weight_sent,) = whole_call(
        piece_rows,
        [jax.ShapeDtypeStruct((PIECE, width), BF)],
        1024 * 1024,
        after(piece.astype(jnp.int32)[None], one),
        near_first,
        return_projection_matrix,
        jnp.pad(after(hidden_shift_vector, one), (0, width - hidden))[None, :],
        scalars=1,
        vmem=54,
    )
    weight_piece = z_mirror(weight_sent)
    raw_image = raw_image_embedding[0]
    raw_blocks = raw_image.reshape(8, rows, width)
    swaps = (core_swap(two), core_swap(one), core_swap(after(three, far)))
    blocks = (own_text, two, one, three, far) + swaps
    factor_row = standardize_factor[None, :]

    def half_rows(value, half):
        halves = value.reshape((4, 2, rows) + value.shape[1:])
        return lax.dynamic_index_in_dim(halves, half, 1, keepdims=False).reshape((4 * rows,) + value.shape[1:])

    base = jnp.stack([(x * 2 + zh) * rows, lax.axis_index("core"), zh]).astype(jnp.int32)
    scalars = (sharpness_factor, similarity_shift, base)
    half_shape = (4 * rows, width)
    pair_flops = 4 * half_shape[0] * 8 * rows * width
    (away_part,) = pair_call(first_pairs, (half_shape,), pair_flops, 20, *scalars, raw_blocks, matching_caption_slot, *blocks)
    away_sum = lax.all_to_all(away_part, "x", 0, 0, tiled=True)
    near_part, even_part, odd_part = pair_call(
        second_pairs,
        (half_shape, half_shape, half_shape),
        2 * pair_flops,
        54,
        *scalars,
        raw_blocks,
        matching_caption_slot,
        *blocks,
        away_part,
    )
    weights = lax.all_gather(after(weight_piece, away_part), ("y", "core"), axis=0, tiled=True)
    sent = jnp.sum(after(away_sum, near_part).reshape(4, rows, -1).astype(F32), 0).astype(BF)
    came = z_swap(sent)

    features = after(half_rows(aggregated_picture_vectors[0], zh), sent).astype(F32)
    centred = features - jnp.mean(features, axis=-1, keepdims=True)
    inv_std = lax.rsqrt(jnp.mean(centred * centred, axis=-1, keepdims=True) + EPSILON)
    normalized = centred * inv_std
    layer_in = (normalized * standardize_factor + standardize_shift).astype(BF)
    (near_slope,) = whole_call(
        slope_rows,
        [jax.ShapeDtypeStruct((4 * rows, hidden), F32)],
        20 * 1024**3,
        layer_in,
        near_first,
        hidden_shift_vector[None, :],
        vmem=54,
    )
    own_raw = rows_of(raw_image, (x * 2 + zh) * rows, rows)
    near_sum = lax.all_to_all(after(near_part, layer_in, own_raw), "x", 0, 0, tiled=True)

    met = even_part.astype(F32) + outer_back(odd_part).astype(F32)
    met_sent = met[2 * rows :].astype(BF)
    came, normalized, near_slope, layer_in = lax.optimization_barrier((came, normalized, near_slope, layer_in))
    came = after(came, met_sent)
    pair_met = met[: 2 * rows] + ring_shift(met_sent, -1).astype(F32)
    pair_sent = pair_met[rows:].astype(BF)

    upstream, spread = whole_call(
        upstream_rows,
        [jax.ShapeDtypeStruct((rows, width), F32), jax.ShapeDtypeStruct(half_shape, BF)],
        1024 * 1024,
        near_sum,
        came,
        own_raw,
    )
    upstream_bf = lax.all_to_all(spread, "x", 0, 0, tiled=True)

    upstream_bf, pair_sent = lax.optimization_barrier((upstream_bf, pair_sent))
    (ln_part,) = whole_call(
        mlp_back,
        [jax.ShapeDtypeStruct(half_shape, BF)],
        8 * 4 * rows * HALF * width,
        upstream_bf,
        factor_row,
        inv_std,
        fetched=(
            return_projection_matrix,
            near_slope,
            layer_in,
            weights,
            near_first,
            normalized,
        ),
        vmem=58,
    )
    parts_x = lax.all_to_all(ln_part, "x", 0, 0, tiled=True)
    d_pooled = upstream + jnp.sum(parts_x.reshape(4, rows, -1).astype(F32), 0)

    (d_text,) = whole_call(
        text_back,
        [jax.ShapeDtypeStruct((rows, width), BF)],
        1,
        pair_met[:rows],
        ring_shift(after(pair_sent, ln_part), -2),
        raw_text,
    )
    return (d_pooled.astype(BF)[None], d_text[None])


def solution(mesh):
    fine = Mesh(mesh.devices.reshape([size for _, size in AXES]), [name for name, _ in AXES])
    placed = (
        P(OUTER, None, None),
        P(OUTER, None, None),
        P(OUTER, INNER, None),
        P(OUTER, None),
        P(),
        P(),
        P(None, INNER),
        P(INNER),
        P(INNER, None),
        P(),
        P(),
    )
    return jax.shard_map(
        local,
        mesh=fine,
        in_specs=placed,
        out_specs=(P(OUTER, INNER, None), P(OUTER, INNER, None)),
        check_vma=False,
    )
```
